32 devices in a mesh: replica: 2 (over y), node: 16 (over z, x, core).
Axes of the slice: x: 2, y: 2, z: 4, core: 2. Of those that a mesh axis runs over, the one named last changes fastest.
Arguments:
- x_rows: bfloat16 [4096, 2048], P(('replica', 'node')), parts along dimension 0, may hold values from -6 to 6
- out_grad: bfloat16 [4096, 2048], P(('replica', 'node')), parts along dimension 0, may hold values from -3 to 3
- expert_ids: int32 [4096, 4], P(('replica', 'node')), parts along dimension 0, may hold values from 0 to 7, all different within a row; in each aligned block of 128 rows (0 to 127, 128 to 255, ...) at most 80 rows name the same one
- gate_values: float32 [4096, 4], P(('replica', 'node')), parts along dimension 0, may hold values from 0.1 to 1
- w_gate: bfloat16 [16, 2048, 384], P('node'), may hold values from -0.125 to 0.125
- w_up: bfloat16 [16, 2048, 384], P('node'), may hold values from -0.125 to 0.125
- w_down: bfloat16 [16, 384, 2048], P('node'), may hold values from -0.21875 to 0.21875
Outputs:
- x_grad: bfloat16 [4096, 2048], P(('replica', 'node')), parts along dimension 0
- gate_grad: float32 [4096, 4], P(('replica', 'node')), parts along dimension 0
- grad_gate: bfloat16 [32, 2048, 384], P(('replica', 'node')), parts along dimension 0
- grad_up: bfloat16 [32, 2048, 384], P(('replica', 'node')), parts along dimension 0
- grad_down: bfloat16 [32, 384, 2048], P(('replica', 'node')), parts along dimension 0
The draws below stay inside these ranges and needn't reach their ends.
There are 2 independent parts, one for each index of `replica`. The reference program is written for one: setup_inputs(seed, part) draws one part's arguments, and reference() takes and returns one part's arrays. A program takes and returns all parts, laid end to end along the dimension named above; an argument that names none is the same for every part. Nothing has to cross between parts.
Inputs may be any that keep to these rules, and one draw needn't show every extreme that they name: `expert_ids`: each row names 4 different experts; within the rows of one device no expert is named more than 80 times, and in some device's rows some expert exactly 80 times.
All inputs are finite; a program needn't handle non-finite values.
Results may differ from the reference program's by a relative error of at most 0.0063.
Values may be sent and summed in bfloat16 or wider, within the bound.
A program may use at most 128 MiB of HBM per device.

```python
import math
import jax
import jax.numpy as jnp
import numpy as np
from jax import lax

D = 2048
H_DEV = 384
TOP = 4
TOK_DEV = 128
EXPERTS = 8
CAP = 80
TOKENS = 2048
N_NODE = 16


def level_of(key, extent, pieces, smallest, largest):
    factor_of, own = 1.0, jax.random.fold_in(key, 6)
    for dim, blocks in pieces:
        heights = jnp.exp(jax.random.uniform(jax.random.fold_in(own, dim), (blocks,), jnp.float32, smallest / len(pieces), largest / len(pieces)))
        factor_of = factor_of * jnp.repeat(heights, extent[dim] // blocks).reshape([-1 if axis == dim else 1 for axis in range(len(extent))])
    return factor_of


def deal_out(key, own, number, rows, count, top, limit, skew):
    sequence = jax.random.permutation(key, count)
    crowded, ordinary = load_shares(count, rows * top, limit, skew, True), load_shares(count, rows * top, limit, skew, False)
    places = jnp.arange(count)

    def named(sizes, rotation):
        used = int((sizes > 0).sum())
        fixed = max(1, used // 4)
        moved = fixed + (places - fixed + rotation * (used - fixed)) % max(1, count - fixed)
        return jnp.zeros((count,), jnp.int32).at[sequence[jnp.where(places < fixed, places, moved)]].set(jnp.asarray(sizes, jnp.int32))

    sizes = jnp.where(number % 4 == 0, named(crowded, number // 4), named(ordinary, number - number // 4 - 1))
    mixed = jax.random.permutation(jax.random.fold_in(own, 3), count)
    donor, receiver = mixed[0:count // 2 * 2:2], mixed[1:count // 2 * 2:2]
    margin = jnp.minimum(sizes[donor] - 1, limit - sizes[receiver]) // 2
    margin = jnp.where((donor == sequence[0]) | (receiver == sequence[0]) | (sizes[receiver] == 0), 0, jnp.maximum(margin, 0))
    moved = jax.random.randint(jax.random.fold_in(own, 4), (count // 2,), 0, 1 << 20) % (margin + 1)
    sizes = sizes.at[donor].add(-moved).at[receiver].add(moved)
    items = jnp.searchsorted(jnp.cumsum(sizes), jnp.arange(rows * top), side="right").astype(jnp.int32)
    grid = items.reshape(top, rows).T
    grid = grid[jax.random.permutation(jax.random.fold_in(own, 1), rows)]
    rotation = jax.random.randint(jax.random.fold_in(own, 2), (rows, 1), 0, top)
    return jnp.take_along_axis(grid, (jnp.arange(top)[None, :] + rotation) % top, axis=1)


def load_shares(amount, total, reach, skew, full):
    loads = [(1 << 20) // math.isqrt(grade ** skew) + 1 for grade in range(1, amount + 1)]
    largest = reach if full else min(reach, max(-(-total // amount), total * loads[0] // sum(loads)))
    least = 1 if total - largest >= amount - 1 else 0
    given, surplus = [largest] + [least] * (amount - 1), total - largest - least * (amount - 1)
    while surplus > 0:
        movable = [i for i in range(1, amount) if given[i] < largest] or [i for i in range(1, amount) if given[i] < reach]
        mass, budget = sum([loads[i] for i in movable]), surplus
        for i in movable:
            more = min(reach - given[i], max(1, budget * loads[i] // mass), surplus)
            given[i] = given[i] + more
            surplus = surplus - more
    return np.array(given)


def normal_values(own_key, extent, deviation, bound, cuts=(), kind=jnp.bfloat16):
    gain = level_of(own_key, extent, cuts, -0.22, 0.18) if cuts else 1.0
    entries = jax.random.normal(own_key, extent, jnp.float32) * deviation * gain
    return jnp.minimum(jnp.maximum(entries, -bound), bound).astype(kind)


def setup_inputs(seed: int = 0, part: int = 0) -> dict:
    arg_keys = jax.random.split(jax.random.key(seed), 8)
    part_keys = jax.random.split(jax.random.fold_in(arg_keys[7], part), 8)
    x_rows = normal_values(part_keys[0], (TOKENS, D), 1.0, 6.0, ((0, 16),))
    out_grad = normal_values(part_keys[1], (TOKENS, D), 0.5, 3.0, ((0, 16),))
    expert_ids_keys = jax.random.split(jax.random.fold_in(part_keys[2], 1), TOKENS // TOK_DEV)
    expert_ids_turns = jax.random.permutation(jax.random.fold_in(part_keys[2], 3), TOKENS // TOK_DEV)
    expert_ids = jax.vmap(lambda own, number: deal_out(jax.random.fold_in(part_keys[2], 2), own, number, TOK_DEV, EXPERTS, TOP, CAP, 2))(expert_ids_keys, expert_ids_turns).reshape((TOKENS, TOP))
    gate_values = jnp.clip(0.1 + 0.9 * jax.random.uniform(part_keys[3], (TOKENS, TOP), jnp.float32) ** level_of(part_keys[3], (TOKENS, TOP), ((0, 16),), -0.2, 0.2), 0.1, 1.0)
    w_gate = normal_values(arg_keys[4], (2 * EXPERTS, D, H_DEV), D ** -0.5, 0.125, ((0, 16),))
    w_up = normal_values(arg_keys[5], (2 * EXPERTS, D, H_DEV), D ** -0.5, 0.125, ((0, 16),))
    w_down = normal_values(arg_keys[6], (2 * EXPERTS, H_DEV, D), (2 * H_DEV) ** -0.5, 0.21875, ((0, 16),))
    return dict(x_rows=x_rows, out_grad=out_grad, expert_ids=expert_ids, gate_values=gate_values, w_gate=w_gate, w_up=w_up, w_down=w_down)


def expert_backward(rows_in, rows_grad, rows_gate, gate_mat, up_mat, down_mat):
    contract_rows = (((0,), (0,)), ((), ()))
    contract_cols = (((1,), (1,)), ((), ()))
    pre_gate = jnp.dot(rows_in, gate_mat, preferred_element_type=jnp.float32)
    pre_up = jnp.dot(rows_in, up_mat, preferred_element_type=jnp.float32)
    sigmoid_gate = jax.nn.sigmoid(pre_gate)
    activation = pre_gate * sigmoid_gate
    hidden = (activation * pre_up).astype(jnp.bfloat16)
    upstream = lax.dot_general(rows_grad, down_mat, contract_cols, preferred_element_type=jnp.float32)
    gate_part = jnp.sum(hidden.astype(jnp.float32) * upstream, axis=1)
    grad_hidden = rows_gate[:, None] * upstream
    grad_pre_gate = (grad_hidden * pre_up * sigmoid_gate * (1.0 + pre_gate * (1.0 - sigmoid_gate))).astype(jnp.bfloat16)
    grad_pre_up = (grad_hidden * activation).astype(jnp.bfloat16)
    scaled_grad = (rows_gate[:, None] * rows_grad.astype(jnp.float32)).astype(jnp.bfloat16)
    down_grad = lax.dot_general(hidden, scaled_grad, contract_rows, preferred_element_type=jnp.float32).astype(jnp.bfloat16)
    gate_mat_grad = lax.dot_general(rows_in, grad_pre_gate, contract_rows, preferred_element_type=jnp.float32).astype(jnp.bfloat16)
    up_mat_grad = lax.dot_general(rows_in, grad_pre_up, contract_rows, preferred_element_type=jnp.float32).astype(jnp.bfloat16)
    input_part = lax.dot_general(grad_pre_gate, gate_mat, contract_cols, preferred_element_type=jnp.float32)
    input_part = input_part + lax.dot_general(grad_pre_up, up_mat, contract_cols, preferred_element_type=jnp.float32)
    return gate_mat_grad, up_mat_grad, down_grad, input_part, gate_part


def reference(x_rows, out_grad, expert_ids, gate_values, w_gate, w_up, w_down):
    count = TOKENS * TOP
    blocks = expert_ids.reshape(N_NODE, TOK_DEV * TOP).astype(jnp.int32)
    one_hot = (blocks[:, :, None] == jnp.arange(EXPERTS, dtype=jnp.int32)[None, None, :]).astype(jnp.int32)
    earlier = jnp.cumsum(one_hot, axis=1) - one_hot
    slot_index = jnp.sum(earlier * one_hot, axis=2).astype(jnp.int32)
    source = jnp.broadcast_to(jnp.arange(N_NODE, dtype=jnp.int32)[:, None], blocks.shape)
    position = ((blocks * N_NODE + source) * CAP + slot_index).reshape(-1).astype(jnp.int32)
    table = jnp.full((EXPERTS * N_NODE * CAP,), count, jnp.int32)
    table = table.at[position].set(jnp.arange(count, dtype=jnp.int32)).reshape(EXPERTS, N_NODE * CAP)
    zero_row = jnp.zeros((1, D), jnp.bfloat16)
    padded_in = jnp.concatenate([x_rows, zero_row], axis=0)
    padded_grad = jnp.concatenate([out_grad, zero_row], axis=0)
    gate_round = lax.optimization_barrier(gate_values.reshape(-1).astype(jnp.bfloat16)).astype(jnp.float32)
    padded_gate = jnp.concatenate([gate_round, jnp.zeros((1,), jnp.float32)], axis=0)
    gate_full = w_gate.reshape(EXPERTS, 2, D, H_DEV).transpose(0, 2, 1, 3).reshape(EXPERTS, D, 2 * H_DEV)
    up_full = w_up.reshape(EXPERTS, 2, D, H_DEV).transpose(0, 2, 1, 3).reshape(EXPERTS, D, 2 * H_DEV)
    down_full = w_down.reshape(EXPERTS, 2 * H_DEV, D)

    def one_expert(item):
        index, gate_mat, up_mat, down_mat = item
        token = index // TOP
        return expert_backward(padded_in[token], padded_grad[token], padded_gate[index], gate_mat, up_mat, down_mat)

    gate_mats, up_mats, down_mats, input_parts, gate_parts = lax.map(one_expert, (table, gate_full, up_full, down_full))
    grad_gate = gate_mats.reshape(EXPERTS, D, 2, H_DEV).transpose(0, 2, 1, 3).reshape(2 * EXPERTS, D, H_DEV)
    grad_up = up_mats.reshape(EXPERTS, D, 2, H_DEV).transpose(0, 2, 1, 3).reshape(2 * EXPERTS, D, H_DEV)
    grad_down = down_mats.reshape(2 * EXPERTS, H_DEV, D)
    x_grad = input_parts.reshape(-1, D)[position].reshape(TOKENS, TOP, D).sum(axis=1).astype(jnp.bfloat16)
    gate_grad = gate_parts.reshape(-1)[position].reshape(TOKENS, TOP)
    return x_grad, gate_grad, grad_gate, grad_up, grad_down
```

```python
import functools

import jax
import jax.numpy as jnp
from jax import lax
from jax.experimental import pallas as pl
from jax.experimental.pallas import tpu as pltpu
from jax.sharding import PartitionSpec as P


RING_NODES = 16


def partner(value, axis, bit):
    mask = 2**bit
    pairs = [(source, source ^ mask) for source in range(lax.axis_size(axis))]
    return lax.ppermute(value, axis, pairs)


def expert_backward(rows_in, rows_grad, rows_gate, gate_mat, up_mat, down_mat):
    contract_rows = (((0,), (0,)), ((), ()))
    contract_cols = (((1,), (1,)), ((), ()))
    pre_gate = jnp.dot(rows_in, gate_mat, preferred_element_type=jnp.float32)
    pre_up = jnp.dot(rows_in, up_mat, preferred_element_type=jnp.float32)
    sigmoid_gate = jax.nn.sigmoid(pre_gate)
    activation = pre_gate * sigmoid_gate
    hidden = (activation * pre_up).astype(jnp.bfloat16)
    upstream = lax.dot_general(
        rows_grad, down_mat, contract_cols, preferred_element_type=jnp.float32
    )
    gate_part = jnp.sum(hidden.astype(jnp.float32) * upstream, axis=1)
    grad_hidden = rows_gate[:, None] * upstream
    grad_pre_gate = (
        grad_hidden * pre_up * sigmoid_gate * (1.0 + pre_gate * (1.0 - sigmoid_gate))
    ).astype(jnp.bfloat16)
    grad_pre_up = (grad_hidden * activation).astype(jnp.bfloat16)
    scaled_grad = (rows_gate[:, None] * rows_grad.astype(jnp.float32)).astype(jnp.bfloat16)
    down_grad = lax.dot_general(
        hidden, scaled_grad, contract_rows, preferred_element_type=jnp.float32
    ).astype(jnp.bfloat16)
    gate_mat_grad = lax.dot_general(
        rows_in, grad_pre_gate, contract_rows, preferred_element_type=jnp.float32
    ).astype(jnp.bfloat16)
    up_mat_grad = lax.dot_general(
        rows_in, grad_pre_up, contract_rows, preferred_element_type=jnp.float32
    ).astype(jnp.bfloat16)
    input_part = lax.dot_general(
        grad_pre_gate, gate_mat, contract_cols, preferred_element_type=jnp.float32
    )
    input_part = input_part + lax.dot_general(
        grad_pre_up, up_mat, contract_cols, preferred_element_type=jnp.float32
    )
    return (gate_mat_grad, up_mat_grad, down_grad, input_part, gate_part)


def exchange_local(x_rows, out_grad, expert_ids, gate_values, w_gate, w_up, w_down):
    nodes = lax.axis_size("node")
    experts = nodes // 2
    tok_rows, width = x_rows.shape
    top_count = expert_ids.shape[1]
    capacity = 2 * max(1, 5 * tok_rows * top_count // (8 * experts))
    half_cap = capacity // 2
    flat_ids = expert_ids.reshape(-1)
    one_hot = (flat_ids[:, None] == jnp.arange(experts, dtype=jnp.int32)[None, :]).astype(jnp.int32)
    earlier = jnp.cumsum(one_hot, axis=0) - one_hot
    slot_index = jnp.sum(earlier * one_hot, axis=1)
    send_place = flat_ids * capacity + slot_index
    send_in = (
        jnp.zeros((experts * capacity, width), jnp.bfloat16)
        .at[send_place]
        .set(jnp.repeat(x_rows, top_count, axis=0))
    )
    send_grad = (
        jnp.zeros((experts * capacity, width), jnp.bfloat16)
        .at[send_place]
        .set(jnp.repeat(out_grad, top_count, axis=0))
    )
    send_gate = (
        jnp.zeros((experts * capacity,), jnp.bfloat16)
        .at[send_place]
        .set(gate_values.reshape(-1).astype(jnp.bfloat16))
    )
    gate_mat = w_gate[0]
    up_mat = w_up[0]
    down_mat = w_down[0]
    mine_in, mine_grad, mine_gate = (
        lax.all_to_all(
            send_in.reshape(nodes, half_cap, width), "node", split_axis=0, concat_axis=0, tiled=True
        ),
        lax.all_to_all(
            send_grad.reshape(nodes, half_cap, width),
            "node",
            split_axis=0,
            concat_axis=0,
            tiled=True,
        ),
        lax.all_to_all(
            send_gate.reshape(nodes, half_cap), "node", split_axis=0, concat_axis=0, tiled=True
        ),
    )
    other_in, other_grad, other_gate = partner((mine_in, mine_grad, mine_gate), "node", 0)
    rows_in = jnp.concatenate([mine_in, other_in], axis=1).reshape(-1, width)
    rows_grad = jnp.concatenate([mine_grad, other_grad], axis=1).reshape(-1, width)
    rows_gate = jnp.concatenate([mine_gate, other_gate], axis=1).reshape(-1).astype(jnp.float32)
    gate_mat_grad, up_mat_grad, down_grad, input_part, gate_part = expert_backward(
        rows_in, rows_grad, rows_gate, gate_mat, up_mat, down_mat
    )
    input_part = input_part.reshape(nodes, capacity, width)
    gate_part = gate_part.reshape(nodes, capacity)
    partner_input, partner_gate = partner(
        (input_part[:, half_cap:], gate_part[:, half_cap:]), "node", 0
    )
    own_input = input_part[:, :half_cap] + partner_input
    own_gate = gate_part[:, :half_cap] + partner_gate
    back_input, back_gate = (
        lax.all_to_all(own_input, "node", split_axis=0, concat_axis=0, tiled=True),
        lax.all_to_all(own_gate, "node", split_axis=0, concat_axis=0, tiled=True),
    )
    summed_input = back_input.reshape(-1, width)
    summed_gate = back_gate.reshape(-1)
    x_grad = (
        summed_input[send_place]
        .reshape(tok_rows, top_count, width)
        .sum(axis=1)
        .astype(jnp.bfloat16)
    )
    gate_grad = summed_gate[send_place].reshape(tok_rows, top_count)
    return (x_grad, gate_grad, gate_mat_grad[None], up_mat_grad[None], down_grad[None])


def ring_kernel(
    nodes,
    x_hbm,
    g_hbm,
    gt_hbm,
    wg_hbm,
    wu_hbm,
    wd_hbm,
    dx_hbm,
    gg_hbm,
    dwg_hbm,
    dwu_hbm,
    dwd_hbm,
    tok,
    gates,
    w_mat,
    wd_mat,
    acc_in,
    acc_down,
    upstream,
    grad_pre,
    hidden,
    gate_col,
    gate_part,
    dx_part,
    home,
    ring_sum,
    side_recv,
    side_send,
    ring_gate,
    side_gate_recv,
    side_gate_send,
    gate_rows,
    home_gate,
    dx_out,
    load_sem,
    tok_ring_send,
    tok_ring_recv,
    tok_side_send,
    tok_side_recv,
    gates_ring_send,
    gates_ring_recv,
    gates_side_send,
    gates_side_recv,
    sum_ring_send,
    sum_ring_recv,
    sum_side_send,
    sum_side_recv,
    gsum_ring_send,
    gsum_ring_recv,
    gsum_side_send,
    gsum_side_recv,
):
    chips = nodes // 2
    depth = chips // 2
    rows, width = x_hbm.shape
    lanes = 128
    tiles = wg_hbm.shape[2] // lanes
    cols = 512
    me = lax.axis_index("node")
    core = me % 2
    mate = 1 - core
    chip = me // 2
    side = chip % 2
    place = chip // 2 + side * (2 * depth - 1 - 2 * (chip // 2))

    def node_at(where):
        where = (where + chips) % chips
        row = where // depth
        level = where + row * (2 * depth - 1 - 2 * where)
        return (level * 2 + row) * 2 + core

    step_dir = 1 - 2 * core
    ahead = {"node": node_at(place + step_dir)}
    behind = {"node": node_at(place - step_dir)}
    other = {"node": chip * 2 + mate}

    loads = [
        (x_hbm, tok.at[0, 0, core]),
        (g_hbm, tok.at[0, 1, core]),
        (gt_hbm, gates.at[0, core]),
        (wd_hbm.at[0], wd_mat),
    ]
    for j in range(tiles):
        part = pl.ds(j * lanes, lanes)
        loads.append((wg_hbm.at[0, :, part], w_mat.at[j, :, pl.ds(0, lanes)]))
        loads.append((wu_hbm.at[0, :, part], w_mat.at[j, :, pl.ds(lanes, lanes)]))
    loads = [
        pltpu.make_async_copy(source, target, load_sem.at[i])
        for i, (source, target) in enumerate(loads)
    ]
    for load in loads:
        load.start()

    barrier = pltpu.get_barrier_semaphore()
    for target in (ahead, behind, other):
        pl.semaphore_signal(barrier, inc=1, device_id=target, device_id_type=pl.DeviceIdType.MESH)
    pl.semaphore_wait(barrier, 3)

    def remote(source, target, send, recv, device):
        return pltpu.make_async_remote_copy(
            src_ref=source,
            dst_ref=target,
            send_sem=send,
            recv_sem=recv,
            device_id=device,
            device_id_type=pl.DeviceIdType.MESH,
        )

    def tok_ring(s):
        return (
            remote(
                tok.at[s, :, core],
                tok.at[s + 1, :, core],
                tok_ring_send.at[s],
                tok_ring_recv.at[s + 1],
                ahead,
            ),
            remote(
                gates.at[s, core],
                gates.at[s + 1, core],
                gates_ring_send.at[s],
                gates_ring_recv.at[s + 1],
                ahead,
            ),
        )

    def tok_side(s, whose):
        return (
            remote(
                tok.at[s, :, whose],
                tok.at[s, :, whose],
                tok_side_send.at[s],
                tok_side_recv.at[s],
                other,
            ),
            remote(
                gates.at[s, whose],
                gates.at[s, whose],
                gates_side_send.at[s],
                gates_side_recv.at[s],
                other,
            ),
        )

    def sum_ring(s):
        return (
            remote(
                ring_sum.at[s],
                ring_sum.at[s + 1],
                sum_ring_send.at[s],
                sum_ring_recv.at[s + 1],
                ahead,
            ),
            remote(
                ring_gate.at[s],
                ring_gate.at[s + 1],
                gsum_ring_send.at[s],
                gsum_ring_recv.at[s + 1],
                ahead,
            ),
        )

    def sum_side(s):
        return (
            remote(
                side_send.at[s], side_recv.at[s], sum_side_send.at[s], sum_side_recv.at[s], other
            ),
            remote(
                side_gate_send.at[s],
                side_gate_recv.at[s],
                gsum_side_send.at[s],
                gsum_side_recv.at[s],
                other,
            ),
        )

    for load in loads[:3]:
        load.wait()

    acc_in[...] = jnp.zeros_like(acc_in)
    acc_down[...] = jnp.zeros_like(acc_down)
    contract_last = (((1,), (1,)), ((), ()))
    contract_first = (((0,), (0,)), ((), ()))
    slots = gates.shape[2]

    def step(s, carry):
        @pl.when(s >= 1)
        def _():
            for copy in tok_ring(s - 1):
                copy.wait_recv()

        @pl.when(s < chips - 1)
        def _():
            for copy in tok_ring(s):
                copy.start()

        for copy in tok_side(s, core):
            copy.start()

        @pl.when(s == 0)
        def _():
            for load in loads[3:]:
                load.wait()

        for copy in tok_side(s, mate):
            copy.wait_recv()

        pick = (lax.broadcasted_iota(jnp.int32, (slots, lanes), 0) == chip).astype(jnp.bfloat16)
        for c in range(2):
            gate_col[c * rows : (c + 1) * rows, :] = lax.dot_general(
                gates[s, c], pick, contract_first, preferred_element_type=jnp.float32
            )
        gate = gate_col[...]

        up = lax.dot_general(
            tok[s, 1].reshape(2 * rows, width),
            wd_mat[...],
            contract_last,
            preferred_element_type=jnp.float32,
        )
        for j in range(tiles):
            upstream[j] = up[:, j * lanes : (j + 1) * lanes]
        gate_part[...] = jnp.zeros_like(gate_part)

        @pl.loop(0, tiles)
        def _(j):
            pre = jnp.dot(
                tok[s, 0].reshape(2 * rows, width), w_mat[j], preferred_element_type=jnp.float32
            )
            pre_gate, pre_up = pre[:, :lanes], pre[:, lanes:]
            sig = jax.nn.sigmoid(pre_gate)
            act = pre_gate * sig
            hid = (act * pre_up).astype(jnp.bfloat16)
            ups = upstream[j]
            gate_part[...] += hid.astype(jnp.float32) * ups
            grad_hidden = gate_col[...] * ups
            grad_pre[j, :, :lanes] = (
                grad_hidden * pre_up * sig * (1.0 + pre_gate * (1.0 - sig))
            ).astype(jnp.bfloat16)
            grad_pre[j, :, lanes:] = (grad_hidden * act).astype(jnp.bfloat16)
            hidden[j] = hid

        @pl.loop(0, width // cols)
        def _(n):
            at = pl.ds(pl.multiple_of(n * cols, cols), cols)
            total = None
            for j in range(tiles):
                term = lax.dot_general(
                    grad_pre[j], w_mat[j, at, :], contract_last, preferred_element_type=jnp.float32
                )
                total = term if total is None else total + term
            dx_part[0, :, at] = total[:rows]
            dx_part[1, :, at] = total[rows:]

        for c in range(2):
            column = jnp.sum(gate_part[c * rows : (c + 1) * rows, :], axis=1, keepdims=True)
            across = jnp.transpose(jnp.broadcast_to(column, (rows, lanes)))[:slots]
            mine = lax.broadcasted_iota(jnp.int32, (slots, rows), 0) == chip
            gate_rows[c] = jnp.where(mine, across, 0.0)

        side_send[s] = dx_part[mate].astype(jnp.bfloat16)
        side_gate_send[s] = gate_rows[mate]
        for copy in sum_side(s):
            copy.start()
        for copy in sum_side(s):
            copy.wait_recv()

        @pl.when(s == 0)
        def _():
            home[...] = dx_part[core] + side_recv[s].astype(jnp.float32)
            home_gate[...] = gate_rows[core] + side_gate_recv[s]

        @pl.when(s == 1)
        def _():
            ring_sum[s] = (dx_part[core] + side_recv[s].astype(jnp.float32)).astype(jnp.bfloat16)
            ring_gate[s] = gate_rows[core] + side_gate_recv[s]

        @pl.when(s >= 2)
        def _():
            for copy in sum_ring(s - 1):
                copy.wait_recv()
            ring_sum[s] = (
                dx_part[core]
                + side_recv[s].astype(jnp.float32)
                + ring_sum[s].astype(jnp.float32)
            ).astype(jnp.bfloat16)
            ring_gate[s] = gate_rows[core] + side_gate_recv[s] + ring_gate[s]

        @pl.when(s >= 1)
        def _():
            for copy in sum_ring(s):
                copy.start()

        @pl.loop(0, width // cols)
        def _(n):
            at = pl.ds(pl.multiple_of(n * cols, cols), cols)
            x_tile = tok[s, 0, :, :, at].reshape(2 * rows, cols)
            g_tile = tok[s, 1, :, :, at].reshape(2 * rows, cols).astype(jnp.float32)
            scaled = jnp.concatenate(
                [
                    (g_tile[:, k * lanes : (k + 1) * lanes] * gate_col[...]).astype(jnp.bfloat16)
                    for k in range(cols // lanes)
                ],
                axis=1,
            )
            for j in range(tiles):
                acc_in[j, at, :] += lax.dot_general(
                    x_tile, grad_pre[j], contract_first, preferred_element_type=jnp.float32
                )
                acc_down[j, :, at] += lax.dot_general(
                    hidden[j], scaled, contract_first, preferred_element_type=jnp.float32
                )

        return carry

    lax.fori_loop(0, chips, step, 0)

    for j in range(tiles):
        w_mat[j] = acc_in[j].astype(jnp.bfloat16)
        wd_mat[j * lanes : (j + 1) * lanes, :] = acc_down[j].astype(jnp.bfloat16)
    stores = [(wd_mat, dwd_hbm.at[0])]
    for j in range(tiles):
        part = pl.ds(j * lanes, lanes)
        stores.append((w_mat.at[j, :, pl.ds(0, lanes)], dwg_hbm.at[0, :, part]))
        stores.append((w_mat.at[j, :, pl.ds(lanes, lanes)], dwu_hbm.at[0, :, part]))
    stores = [
        pltpu.make_async_copy(source, target, load_sem.at[i])
        for i, (source, target) in enumerate(stores)
    ]
    for store in stores:
        store.start()

    for copy in sum_ring(chips - 1):
        copy.wait_recv()
    dx_out[...] = (home[...] + ring_sum[chips].astype(jnp.float32)).astype(jnp.bfloat16)
    home_gate[...] += ring_gate[chips]
    last = [
        pltpu.make_async_copy(dx_out, dx_hbm, load_sem.at[len(stores)]),
        pltpu.make_async_copy(home_gate, gg_hbm, load_sem.at[len(stores) + 1]),
    ]
    for store in last:
        store.start()

    def drain(s, carry):
        @pl.when(s < chips - 1)
        def _():
            for copy in tok_ring(s):
                copy.wait_send()

        @pl.when(s >= 1)
        def _():
            for copy in sum_ring(s):
                copy.wait_send()

        for copy in tok_side(s, core):
            copy.wait_send()
        for copy in sum_side(s):
            copy.wait_send()
        return carry

    lax.fori_loop(0, chips, drain, 0)
    for store in stores + last:
        store.wait()


def ring_local(x_rows, out_grad, expert_ids, gate_values, w_gate, w_up, w_down):
    nodes = lax.axis_size("node")
    chips = nodes // 2
    rows, width = x_rows.shape
    hid = w_gate.shape[2]
    lanes = 128
    tiles = hid // lanes
    slots = (chips + 15) // 16 * 16
    expert = jnp.arange(slots, dtype=jnp.int32)[:, None]
    named = [expert == expert_ids[:, k][None, :] for k in range(expert_ids.shape[1])]
    gate_table = sum(
        jnp.where(named[k], gate_values[:, k][None, :], 0.0) for k in range(len(named))
    ).astype(jnp.bfloat16)
    any_space = pl.BlockSpec(memory_space=pl.ANY)
    bf16, f32 = jnp.bfloat16, jnp.float32
    dma = pltpu.SemaphoreType.DMA
    flops = 2 * nodes * rows * width * hid * 8
    x_grad, gate_sum, d_gate, d_up, d_down = pl.pallas_call(
        functools.partial(ring_kernel, nodes),
        out_shape=(
            jax.ShapeDtypeStruct((rows, width), bf16),
            jax.ShapeDtypeStruct((slots, rows), f32),
            jax.ShapeDtypeStruct((1, width, hid), bf16),
            jax.ShapeDtypeStruct((1, width, hid), bf16),
            jax.ShapeDtypeStruct((1, hid, width), bf16),
        ),
        in_specs=[any_space] * 6,
        out_specs=(any_space,) * 5,
        scratch_shapes=[
            pltpu.VMEM((chips, 2, 2, rows, width), bf16),
            pltpu.VMEM((chips, 2, slots, rows), bf16),
            pltpu.VMEM((tiles, width, 2 * lanes), bf16),
            pltpu.VMEM((hid, width), bf16),
            pltpu.VMEM((tiles, width, 2 * lanes), f32),
            pltpu.VMEM((tiles, lanes, width), f32),
            pltpu.VMEM((tiles, 2 * rows, lanes), f32),
            pltpu.VMEM((tiles, 2 * rows, 2 * lanes), bf16),
            pltpu.VMEM((tiles, 2 * rows, lanes), bf16),
            pltpu.VMEM((2 * rows, lanes), f32),
            pltpu.VMEM((2 * rows, lanes), f32),
            pltpu.VMEM((2, rows, width), f32),
            pltpu.VMEM((rows, width), f32),
            pltpu.VMEM((chips + 1, rows, width), bf16),
            pltpu.VMEM((chips, rows, width), bf16),
            pltpu.VMEM((chips, rows, width), bf16),
            pltpu.VMEM((chips + 1, slots, rows), f32),
            pltpu.VMEM((chips, slots, rows), f32),
            pltpu.VMEM((chips, slots, rows), f32),
            pltpu.VMEM((2, slots, rows), f32),
            pltpu.VMEM((slots, rows), f32),
            pltpu.VMEM((rows, width), bf16),
            dma((4 + 2 * tiles,)),
        ]
        + [dma((chips + 1,))] * 16,
        compiler_params=pltpu.CompilerParams(
            collective_id=0, has_side_effects=True, vmem_limit_bytes=60 * 2**20
        ),
        cost_estimate=pl.CostEstimate(
            flops=flops, bytes_accessed=12 * width * hid, transcendentals=nodes * rows * hid
        ),
    )(x_rows, out_grad, gate_table, w_gate, w_up, w_down)
    gate_grad = jnp.stack(
        [jnp.sum(jnp.where(chosen, gate_sum, 0.0), axis=0) for chosen in named], axis=1
    )
    return (x_grad, gate_grad, d_gate, d_up, d_down)


def solution(mesh):
    local = ring_local if mesh.shape["node"] <= RING_NODES else exchange_local
    return jax.shard_map(
        local,
        mesh=mesh,
        in_specs=(
            P(("replica", "node"), None),
            P(("replica", "node"), None),
            P(("replica", "node"), None),
            P(("replica", "node"), None),
            P("node", None, None),
            P("node", None, None),
            P("node", None, None),
        ),
        out_specs=(
            P(("replica", "node"), None),
            P(("replica", "node"), None),
            P(("replica", "node"), None, None),
            P(("replica", "node"), None, None),
            P(("replica", "node"), None, None),
        ),
        check_vma=False,
    )
```

```python
import functools

import jax
import jax.numpy as jnp
from jax import lax
from jax.experimental import pallas as pl
from jax.experimental.pallas import tpu as pltpu
from jax.sharding import PartitionSpec as P


RING_NODES = 16


def partner(value, axis, bit):
    mask = 2**bit
    pairs = [(source, source ^ mask) for source in range(lax.axis_size(axis))]
    return lax.ppermute(value, axis, pairs)


def expert_backward(rows_in, rows_grad, rows_gate, gate_mat, up_mat, down_mat):
    contract_rows = (((0,), (0,)), ((), ()))
    contract_cols = (((1,), (1,)), ((), ()))
    pre_gate = jnp.dot(rows_in, gate_mat, preferred_element_type=jnp.float32)
    pre_up = jnp.dot(rows_in, up_mat, preferred_element_type=jnp.float32)
    sigmoid_gate = jax.nn.sigmoid(pre_gate)
    activation = pre_gate * sigmoid_gate
    hidden = (activation * pre_up).astype(jnp.bfloat16)
    upstream = lax.dot_general(
        rows_grad, down_mat, contract_cols, preferred_element_type=jnp.float32
    )
    gate_part = jnp.sum(hidden.astype(jnp.float32) * upstream, axis=1)
    grad_hidden = rows_gate[:, None] * upstream
    grad_pre_gate = (
        grad_hidden * pre_up * sigmoid_gate * (1.0 + pre_gate * (1.0 - sigmoid_gate))
    ).astype(jnp.bfloat16)
    grad_pre_up = (grad_hidden * activation).astype(jnp.bfloat16)
    scaled_grad = (rows_gate[:, None] * rows_grad.astype(jnp.float32)).astype(jnp.bfloat16)
    down_grad = lax.dot_general(
        hidden, scaled_grad, contract_rows, preferred_element_type=jnp.float32
    ).astype(jnp.bfloat16)
    gate_mat_grad = lax.dot_general(
        rows_in, grad_pre_gate, contract_rows, preferred_element_type=jnp.float32
    ).astype(jnp.bfloat16)
    up_mat_grad = lax.dot_general(
        rows_in, grad_pre_up, contract_rows, preferred_element_type=jnp.float32
    ).astype(jnp.bfloat16)
    input_part = lax.dot_general(
        grad_pre_gate, gate_mat, contract_cols, preferred_element_type=jnp.float32
    )
    input_part = input_part + lax.dot_general(
        grad_pre_up, up_mat, contract_cols, preferred_element_type=jnp.float32
    )
    return (gate_mat_grad, up_mat_grad, down_grad, input_part, gate_part)


def exchange_local(x_rows, out_grad, expert_ids, gate_values, w_gate, w_up, w_down):
    nodes = lax.axis_size("node")
    experts = nodes // 2
    tok_rows, width = x_rows.shape
    top_count = expert_ids.shape[1]
    capacity = 2 * max(1, 5 * tok_rows * top_count // (8 * experts))
    half_cap = capacity // 2
    flat_ids = expert_ids.reshape(-1)
    one_hot = (flat_ids[:, None] == jnp.arange(experts, dtype=jnp.int32)[None, :]).astype(jnp.int32)
    earlier = jnp.cumsum(one_hot, axis=0) - one_hot
    slot_index = jnp.sum(earlier * one_hot, axis=1)
    send_place = flat_ids * capacity + slot_index
    send_in = (
        jnp.zeros((experts * capacity, width), jnp.bfloat16)
        .at[send_place]
        .set(jnp.repeat(x_rows, top_count, axis=0))
    )
    send_grad = (
        jnp.zeros((experts * capacity, width), jnp.bfloat16)
        .at[send_place]
        .set(jnp.repeat(out_grad, top_count, axis=0))
    )
    send_gate = (
        jnp.zeros((experts * capacity,), jnp.bfloat16)
        .at[send_place]
        .set(gate_values.reshape(-1).astype(jnp.bfloat16))
    )
    gate_mat = w_gate[0]
    up_mat = w_up[0]
    down_mat = w_down[0]
    mine_in, mine_grad, mine_gate = (
        lax.all_to_all(
            send_in.reshape(nodes, half_cap, width), "node", split_axis=0, concat_axis=0, tiled=True
        ),
        lax.all_to_all(
            send_grad.reshape(nodes, half_cap, width),
            "node",
            split_axis=0,
            concat_axis=0,
            tiled=True,
        ),
        lax.all_to_all(
            send_gate.reshape(nodes, half_cap), "node", split_axis=0, concat_axis=0, tiled=True
        ),
    )
    other_in, other_grad, other_gate = partner((mine_in, mine_grad, mine_gate), "node", 0)
    rows_in = jnp.concatenate([mine_in, other_in], axis=1).reshape(-1, width)
    rows_grad = jnp.concatenate([mine_grad, other_grad], axis=1).reshape(-1, width)
    rows_gate = jnp.concatenate([mine_gate, other_gate], axis=1).reshape(-1).astype(jnp.float32)
    gate_mat_grad, up_mat_grad, down_grad, input_part, gate_part = expert_backward(
        rows_in, rows_grad, rows_gate, gate_mat, up_mat, down_mat
    )
    input_part = input_part.reshape(nodes, capacity, width)
    gate_part = gate_part.reshape(nodes, capacity)
    partner_input, partner_gate = partner(
        (input_part[:, half_cap:], gate_part[:, half_cap:]), "node", 0
    )
    own_input = input_part[:, :half_cap] + partner_input
    own_gate = gate_part[:, :half_cap] + partner_gate
    back_input, back_gate = (
        lax.all_to_all(own_input, "node", split_axis=0, concat_axis=0, tiled=True),
        lax.all_to_all(own_gate, "node", split_axis=0, concat_axis=0, tiled=True),
    )
    summed_input = back_input.reshape(-1, width)
    summed_gate = back_gate.reshape(-1)
    x_grad = (
        summed_input[send_place]
        .reshape(tok_rows, top_count, width)
        .sum(axis=1)
        .astype(jnp.bfloat16)
    )
    gate_grad = summed_gate[send_place].reshape(tok_rows, top_count)
    return (x_grad, gate_grad, gate_mat_grad[None], up_mat_grad[None], down_grad[None])


def ring_kernel(
    nodes,
    x_hbm,
    g_hbm,
    gt_hbm,
    wg_hbm,
    wu_hbm,
    wd_hbm,
    dx_hbm,
    gg_hbm,
    dwg_hbm,
    dwu_hbm,
    dwd_hbm,
    tok,
    gates,
    w_mat,
    wd_mat,
    acc_in,
    acc_down,
    upstream,
    grad_pre,
    hidden,
    gate_col,
    gate_part,
    dx_part,
    home,
    own_part,
    own_gate,
    ring_sum,
    side_recv,
    side_send,
    ring_gate,
    side_gate_recv,
    side_gate_send,
    gate_rows,
    home_gate,
    dx_out,
    load_sem,
    tok_ring_send,
    tok_ring_recv,
    tok_side_send,
    tok_side_recv,
    gates_ring_send,
    gates_ring_recv,
    gates_side_send,
    gates_side_recv,
    sum_ring_send,
    sum_ring_recv,
    sum_side_send,
    sum_side_recv,
    gsum_ring_send,
    gsum_ring_recv,
    gsum_side_send,
    gsum_side_recv,
):
    chips = nodes // 2
    depth = chips // 2
    rows, width = x_hbm.shape
    lanes = 128
    tiles = wg_hbm.shape[2] // lanes
    cols = 512
    me = lax.axis_index("node")
    core = me % 2
    mate = 1 - core
    chip = me // 2
    side = chip % 2
    place = chip // 2 + side * (2 * depth - 1 - 2 * (chip // 2))

    def node_at(where):
        where = (where + chips) % chips
        row = where // depth
        level = where + row * (2 * depth - 1 - 2 * where)
        return (level * 2 + row) * 2 + core

    step_dir = 1 - 2 * core
    ahead = {"node": node_at(place + step_dir)}
    behind = {"node": node_at(place - step_dir)}
    other = {"node": chip * 2 + mate}

    loads = [
        (x_hbm, tok.at[0, 0, core]),
        (g_hbm, tok.at[0, 1, core]),
        (gt_hbm, gates.at[0, core]),
        (wd_hbm.at[0], wd_mat),
    ]
    for j in range(tiles):
        part = pl.ds(j * lanes, lanes)
        loads.append((wg_hbm.at[0, :, part], w_mat.at[j, :, pl.ds(0, lanes)]))
        loads.append((wu_hbm.at[0, :, part], w_mat.at[j, :, pl.ds(lanes, lanes)]))
    loads = [
        pltpu.make_async_copy(source, target, load_sem.at[i])
        for i, (source, target) in enumerate(loads)
    ]
    for load in loads:
        load.start()

    barrier = pltpu.get_barrier_semaphore()
    for target in (ahead, behind, other):
        pl.semaphore_signal(barrier, inc=1, device_id=target, device_id_type=pl.DeviceIdType.MESH)
    pl.semaphore_wait(barrier, 3)

    def remote(source, target, send, recv, device):
        return pltpu.make_async_remote_copy(
            src_ref=source,
            dst_ref=target,
            send_sem=send,
            recv_sem=recv,
            device_id=device,
            device_id_type=pl.DeviceIdType.MESH,
        )

    def tok_ring(s, kind):
        return remote(
            tok.at[s, kind, core],
            tok.at[s + 1, kind, core],
            tok_ring_send.at[s, kind],
            tok_ring_recv.at[s + 1, kind],
            ahead,
        )

    def gates_ring(s):
        return remote(
            gates.at[s, core],
            gates.at[s + 1, core],
            gates_ring_send.at[s],
            gates_ring_recv.at[s + 1],
            ahead,
        )

    def tok_side(s, kind, whose):
        return remote(
            tok.at[s, kind, whose],
            tok.at[s, kind, whose],
            tok_side_send.at[s, kind],
            tok_side_recv.at[s, kind],
            other,
        )

    def gates_side(s, whose):
        return remote(
            gates.at[s, whose],
            gates.at[s, whose],
            gates_side_send.at[s],
            gates_side_recv.at[s],
            other,
        )

    half = width // 2

    def sum_ring(s, h):
        return remote(
            ring_sum.at[s, h],
            ring_sum.at[s + 1, h],
            sum_ring_send.at[s, h],
            sum_ring_recv.at[s + 1, h],
            ahead,
        )

    def gsum_ring(s):
        return remote(
            ring_gate.at[s],
            ring_gate.at[s + 1],
            gsum_ring_send.at[s],
            gsum_ring_recv.at[s + 1],
            ahead,
        )

    def sum_side(s):
        return (
            remote(
                side_send.at[s], side_recv.at[s], sum_side_send.at[s], sum_side_recv.at[s], other
            ),
            remote(
                side_gate_send.at[s],
                side_gate_recv.at[s],
                gsum_side_send.at[s],
                gsum_side_recv.at[s],
                other,
            ),
        )

    for load in loads[:3]:
        load.wait()

    contract_last = (((1,), (1,)), ((), ()))
    contract_first = (((0,), (0,)), ((), ()))
    slots = gates.shape[2]

    lag = 2
    kept = own_part.shape[0]

    def add_and_send(s):
        for copy in sum_side(s):
            copy.wait_recv()
        gates_total = own_gate[s % kept] + side_gate_recv[s]

        @pl.when(s == 1)
        def _():
            ring_gate[s] = gates_total

        @pl.when(s >= 2)
        def _():
            gsum_ring(s - 1).wait_recv()
            ring_gate[s] = gates_total + ring_gate[s]

        gsum_ring(s).start()
        for h in range(2):
            part = slice(h * half, (h + 1) * half)

            @pl.when(s == 1)
            def _():
                ring_sum[s, h] = (
                    own_part[s % kept, h] + side_recv[s, :, part].astype(jnp.float32)
                ).astype(jnp.bfloat16)

            @pl.when(s >= 2)
            def _():
                sum_ring(s - 1, h).wait_recv()
                ring_sum[s, h] = (
                    own_part[s % kept, h]
                    + side_recv[s, :, part].astype(jnp.float32)
                    + ring_sum[s, h].astype(jnp.float32)
                ).astype(jnp.bfloat16)

            sum_ring(s, h).start()

    def step(s, carry):
        @pl.when(s >= 1)
        def _():
            gates_ring(s - 1).wait_recv()

        @pl.when(s < chips - 1)
        def _():
            gates_ring(s).start()

        gates_side(s, core).start()
        for kind in (1, 0):

            @pl.when(s >= 1)
            def _():
                tok_ring(s - 1, kind).wait_recv()

            @pl.when(s < chips - 1)
            def _():
                tok_ring(s, kind).start()

            tok_side(s, kind, core).start()

        @pl.when(s == 0)
        def _():
            acc_in[...] = jnp.zeros_like(acc_in)
            acc_down[...] = jnp.zeros_like(acc_down)
            for load in loads[3:]:
                load.wait()

        @pl.when(s >= lag + 1)
        def _():
            add_and_send(s - lag)

        gates_side(s, mate).wait_recv()
        tok_side(s, 1, mate).wait_recv()
        tok_side(s, 0, mate).wait_recv()

        pick = (lax.broadcasted_iota(jnp.int32, (slots, lanes), 0) == chip).astype(jnp.bfloat16)
        for c in range(2):
            gate_col[c * rows : (c + 1) * rows, :] = lax.dot_general(
                gates[s, c], pick, contract_first, preferred_element_type=jnp.float32
            )
        gate = gate_col[...]

        up = lax.dot_general(
            tok[s, 1].reshape(2 * rows, width),
            wd_mat[...],
            contract_last,
            preferred_element_type=jnp.float32,
        )
        for j in range(tiles):
            upstream[j] = up[:, j * lanes : (j + 1) * lanes]
        gate_part[...] = jnp.zeros_like(gate_part)

        @pl.loop(0, tiles)
        def _(j):
            pre = jnp.dot(
                tok[s, 0].reshape(2 * rows, width), w_mat[j], preferred_element_type=jnp.float32
            )
            pre_gate, pre_up = pre[:, :lanes], pre[:, lanes:]
            sig = jax.nn.sigmoid(pre_gate)
            act = pre_gate * sig
            hid = (act * pre_up).astype(jnp.bfloat16)
            ups = upstream[j]
            gate_part[...] += hid.astype(jnp.float32) * ups
            grad_hidden = gate_col[...] * ups
            grad_pre[j, :, :lanes] = (
                grad_hidden * pre_up * sig * (1.0 + pre_gate * (1.0 - sig))
            ).astype(jnp.bfloat16)
            grad_pre[j, :, lanes:] = (grad_hidden * act).astype(jnp.bfloat16)
            hidden[j] = hid

        @pl.loop(0, width // cols)
        def _(n):
            at = pl.ds(pl.multiple_of(n * cols, cols), cols)
            total = None
            for j in range(tiles):
                term = lax.dot_general(
                    grad_pre[j], w_mat[j, at, :], contract_last, preferred_element_type=jnp.float32
                )
                total = term if total is None else total + term
            dx_part[0, :, at] = total[:rows]
            dx_part[1, :, at] = total[rows:]

        for c in range(2):
            column = jnp.sum(gate_part[c * rows : (c + 1) * rows, :], axis=1, keepdims=True)
            across = jnp.transpose(jnp.broadcast_to(column, (rows, lanes)))[:slots]
            mine = lax.broadcasted_iota(jnp.int32, (slots, rows), 0) == chip
            gate_rows[c] = jnp.where(mine, across, 0.0)

        side_send[s] = dx_part[mate].astype(jnp.bfloat16)
        side_gate_send[s] = gate_rows[mate]
        for copy in sum_side(s):
            copy.start()

        @pl.when(s == 0)
        def _():
            for h in range(2):
                home[h] = dx_part[core, :, h * half : (h + 1) * half]
            home_gate[...] = gate_rows[core]

        @pl.when(s >= 1)
        def _():
            for h in range(2):
                own_part[s % kept, h] = dx_part[core, :, h * half : (h + 1) * half]
            own_gate[s % kept] = gate_rows[core]

        @pl.when(s == chips - 1)
        def _():
            for late in range(lag - 1, 0, -1):
                add_and_send(chips - 1 - late)

        @pl.loop(0, width // cols)
        def _(n):
            at = pl.ds(pl.multiple_of(n * cols, cols), cols)
            x_tile = tok[s, 0, :, :, at].reshape(2 * rows, cols)
            g_tile = tok[s, 1, :, :, at].reshape(2 * rows, cols).astype(jnp.float32)
            scaled = jnp.concatenate(
                [
                    (g_tile[:, k * lanes : (k + 1) * lanes] * gate_col[...]).astype(jnp.bfloat16)
                    for k in range(cols // lanes)
                ],
                axis=1,
            )
            for j in range(tiles):
                acc_in[j, at, :] += lax.dot_general(
                    x_tile, grad_pre[j], contract_first, preferred_element_type=jnp.float32
                )
                acc_down[j, :, at] += lax.dot_general(
                    hidden[j], scaled, contract_first, preferred_element_type=jnp.float32
                )

        return carry

    lax.fori_loop(0, chips, step, 0)
    add_and_send(chips - 1)

    for j in range(tiles):
        w_mat[j] = acc_in[j].astype(jnp.bfloat16)
        wd_mat[j * lanes : (j + 1) * lanes, :] = acc_down[j].astype(jnp.bfloat16)
    stores = [(wd_mat, dwd_hbm.at[0])]
    for j in range(tiles):
        part = pl.ds(j * lanes, lanes)
        stores.append((w_mat.at[j, :, pl.ds(0, lanes)], dwg_hbm.at[0, :, part]))
        stores.append((w_mat.at[j, :, pl.ds(lanes, lanes)], dwu_hbm.at[0, :, part]))
    stores = [
        pltpu.make_async_copy(source, target, load_sem.at[i])
        for i, (source, target) in enumerate(stores)
    ]
    for store in stores:
        store.start()

    for copy in sum_side(0):
        copy.wait_recv()
    gsum_ring(chips - 1).wait_recv()
    home_gate[...] += side_gate_recv[0] + ring_gate[chips]
    for h in range(2):
        part = slice(h * half, (h + 1) * half)
        sum_ring(chips - 1, h).wait_recv()
        dx_out[:, part] = (
            home[h] + side_recv[0, :, part].astype(jnp.float32) + ring_sum[chips, h].astype(jnp.float32)
        ).astype(jnp.bfloat16)
    last = [
        pltpu.make_async_copy(dx_out, dx_hbm, load_sem.at[len(stores)]),
        pltpu.make_async_copy(home_gate, gg_hbm, load_sem.at[len(stores) + 1]),
    ]
    for store in last:
        store.start()

    def drain(s, carry):
        @pl.when(s < chips - 1)
        def _():
            gates_ring(s).wait_send()
            for kind in range(2):
                tok_ring(s, kind).wait_send()

        @pl.when(s >= 1)
        def _():
            gsum_ring(s).wait_send()
            for h in range(2):
                sum_ring(s, h).wait_send()

        gates_side(s, core).wait_send()
        for kind in range(2):
            tok_side(s, kind, core).wait_send()
        for copy in sum_side(s):
            copy.wait_send()
        return carry

    lax.fori_loop(0, chips, drain, 0)
    for store in stores + last:
        store.wait()


def hand_over(*refs):
    count = len(refs) // 2
    for source, target in zip(refs[:count], refs[count:]):
        target[...] = source[...]


def ring_local(x_rows, out_grad, expert_ids, gate_values, w_gate, w_up, w_down):
    nodes = lax.axis_size("node")
    chips = nodes // 2
    rows, width = x_rows.shape
    hid = w_gate.shape[2]
    lanes = 128
    tiles = hid // lanes
    slots = (chips + 15) // 16 * 16
    expert = jnp.arange(slots, dtype=jnp.int32)[:, None]
    named = [expert == expert_ids[:, k][None, :] for k in range(expert_ids.shape[1])]
    gate_table = sum(
        jnp.where(named[k], gate_values[:, k][None, :], 0.0) for k in range(len(named))
    ).astype(jnp.bfloat16)
    any_space = pl.BlockSpec(memory_space=pl.ANY)
    bf16, f32 = jnp.bfloat16, jnp.float32
    dma = pltpu.SemaphoreType.DMA
    flops = 2 * nodes * rows * width * hid * 8
    x_grad, gate_sum, d_gate, d_up, d_down = pl.pallas_call(
        functools.partial(ring_kernel, nodes),
        out_shape=(
            jax.ShapeDtypeStruct((rows, width), bf16),
            jax.ShapeDtypeStruct((slots, rows), f32),
            jax.ShapeDtypeStruct((1, width, hid), bf16),
            jax.ShapeDtypeStruct((1, width, hid), bf16),
            jax.ShapeDtypeStruct((1, hid, width), bf16),
        ),
        in_specs=[any_space] * 6,
        out_specs=(any_space,) * 5,
        scratch_shapes=[
            pltpu.VMEM((chips, 2, 2, rows, width), bf16),
            pltpu.VMEM((chips, 2, slots, rows), bf16),
            pltpu.VMEM((tiles, width, 2 * lanes), bf16),
            pltpu.VMEM((hid, width), bf16),
            pltpu.VMEM((tiles, width, 2 * lanes), f32),
            pltpu.VMEM((tiles, lanes, width), f32),
            pltpu.VMEM((tiles, 2 * rows, lanes), f32),
            pltpu.VMEM((tiles, 2 * rows, 2 * lanes), bf16),
            pltpu.VMEM((tiles, 2 * rows, lanes), bf16),
            pltpu.VMEM((2 * rows, lanes), f32),
            pltpu.VMEM((2 * rows, lanes), f32),
            pltpu.VMEM((2, rows, width), f32),
            pltpu.VMEM((2, rows, width // 2), f32),
            pltpu.VMEM((3, 2, rows, width // 2), f32),
            pltpu.VMEM((3, slots, rows), f32),
            pltpu.VMEM((chips + 1, 2, rows, width // 2), bf16),
            pltpu.VMEM((chips, rows, width), bf16),
            pltpu.VMEM((chips, rows, width), bf16),
            pltpu.VMEM((chips + 1, slots, rows), f32),
            pltpu.VMEM((chips, slots, rows), f32),
            pltpu.VMEM((chips, slots, rows), f32),
            pltpu.VMEM((2, slots, rows), f32),
            pltpu.VMEM((slots, rows), f32),
            pltpu.VMEM((rows, width), bf16),
            dma((4 + 2 * tiles,)),
        ]
        + [dma((chips + 1, 2))] * 4
        + [dma((chips + 1,))] * 4
        + [dma((chips + 1, 2))] * 2
        + [dma((chips + 1,))] * 6,
        compiler_params=pltpu.CompilerParams(
            collective_id=0, has_side_effects=True, vmem_limit_bytes=60 * 2**20
        ),
        cost_estimate=pl.CostEstimate(
            flops=flops, bytes_accessed=12 * width * hid, transcendentals=nodes * rows * hid
        ),
    )(x_rows, out_grad, gate_table, w_gate, w_up, w_down)
    results = (x_grad, d_gate, d_up, d_down)
    pieces = 4
    blocks = [
        pl.BlockSpec((rows // pieces, width), lambda i: (i, 0)),
        pl.BlockSpec((1, width // pieces, hid), lambda i: (0, i, 0)),
        pl.BlockSpec((1, width // pieces, hid), lambda i: (0, i, 0)),
        pl.BlockSpec((1, hid // pieces, width), lambda i: (0, i, 0)),
    ]
    x_grad, d_gate, d_up, d_down = pl.pallas_call(
        hand_over,
        grid=(pieces,),
        out_shape=tuple(jax.ShapeDtypeStruct(r.shape, r.dtype) for r in results),
        in_specs=blocks,
        out_specs=tuple(blocks),
    )(*results)
    gate_grad = jnp.stack(
        [jnp.sum(jnp.where(chosen, gate_sum, 0.0), axis=0) for chosen in named], axis=1
    )
    return (x_grad, gate_grad, d_gate, d_up, d_down)


def solution(mesh):
    local = ring_local if mesh.shape["node"] <= RING_NODES else exchange_local
    return jax.shard_map(
        local,
        mesh=mesh,
        in_specs=(
            P(("replica", "node"), None),
            P(("replica", "node"), None),
            P(("replica", "node"), None),
            P(("replica", "node"), None),
            P("node", None, None),
            P("node", None, None),
            P("node", None, None),
        ),
        out_specs=(
            P(("replica", "node"), None),
            P(("replica", "node"), None),
            P(("replica", "node"), None, None),
            P(("replica", "node"), None, None),
            P(("replica", "node"), None, None),
        ),
        check_vma=False,
    )
```

```python
import functools

import jax
import jax.numpy as jnp
from jax import lax
from jax.experimental import pallas as pl
from jax.experimental.pallas import tpu as pltpu
from jax.sharding import PartitionSpec as P


RING_NODES = 16


def partner(value, axis, bit):
    mask = 2**bit
    pairs = [(source, source ^ mask) for source in range(lax.axis_size(axis))]
    return lax.ppermute(value, axis, pairs)


def expert_backward(rows_in, rows_grad, rows_gate, gate_mat, up_mat, down_mat):
    contract_rows = (((0,), (0,)), ((), ()))
    contract_cols = (((1,), (1,)), ((), ()))
    pre_gate = jnp.dot(rows_in, gate_mat, preferred_element_type=jnp.float32)
    pre_up = jnp.dot(rows_in, up_mat, preferred_element_type=jnp.float32)
    sigmoid_gate = jax.nn.sigmoid(pre_gate)
    activation = pre_gate * sigmoid_gate
    hidden = (activation * pre_up).astype(jnp.bfloat16)
    upstream = lax.dot_general(
        rows_grad, down_mat, contract_cols, preferred_element_type=jnp.float32
    )
    gate_part = jnp.sum(hidden.astype(jnp.float32) * upstream, axis=1)
    grad_hidden = rows_gate[:, None] * upstream
    grad_pre_gate = (
        grad_hidden * pre_up * sigmoid_gate * (1.0 + pre_gate * (1.0 - sigmoid_gate))
    ).astype(jnp.bfloat16)
    grad_pre_up = (grad_hidden * activation).astype(jnp.bfloat16)
    scaled_grad = (rows_gate[:, None] * rows_grad.astype(jnp.float32)).astype(jnp.bfloat16)
    down_grad = lax.dot_general(
        hidden, scaled_grad, contract_rows, preferred_element_type=jnp.float32
    ).astype(jnp.bfloat16)
    gate_mat_grad = lax.dot_general(
        rows_in, grad_pre_gate, contract_rows, preferred_element_type=jnp.float32
    ).astype(jnp.bfloat16)
    up_mat_grad = lax.dot_general(
        rows_in, grad_pre_up, contract_rows, preferred_element_type=jnp.float32
    ).astype(jnp.bfloat16)
    input_part = lax.dot_general(
        grad_pre_gate, gate_mat, contract_cols, preferred_element_type=jnp.float32
    )
    input_part = input_part + lax.dot_general(
        grad_pre_up, up_mat, contract_cols, preferred_element_type=jnp.float32
    )
    return (gate_mat_grad, up_mat_grad, down_grad, input_part, gate_part)


def exchange_local(x_rows, out_grad, expert_ids, gate_values, w_gate, w_up, w_down):
    nodes = lax.axis_size("node")
    experts = nodes // 2
    tok_rows, width = x_rows.shape
    top_count = expert_ids.shape[1]
    capacity = 2 * max(1, 5 * tok_rows * top_count // (8 * experts))
    half_cap = capacity // 2
    flat_ids = expert_ids.reshape(-1)
    one_hot = (flat_ids[:, None] == jnp.arange(experts, dtype=jnp.int32)[None, :]).astype(jnp.int32)
    earlier = jnp.cumsum(one_hot, axis=0) - one_hot
    slot_index = jnp.sum(earlier * one_hot, axis=1)
    send_place = flat_ids * capacity + slot_index
    send_in = (
        jnp.zeros((experts * capacity, width), jnp.bfloat16)
        .at[send_place]
        .set(jnp.repeat(x_rows, top_count, axis=0))
    )
    send_grad = (
        jnp.zeros((experts * capacity, width), jnp.bfloat16)
        .at[send_place]
        .set(jnp.repeat(out_grad, top_count, axis=0))
    )
    send_gate = (
        jnp.zeros((experts * capacity,), jnp.bfloat16)
        .at[send_place]
        .set(gate_values.reshape(-1).astype(jnp.bfloat16))
    )
    gate_mat = w_gate[0]
    up_mat = w_up[0]
    down_mat = w_down[0]
    mine_in, mine_grad, mine_gate = (
        lax.all_to_all(
            send_in.reshape(nodes, half_cap, width), "node", split_axis=0, concat_axis=0, tiled=True
        ),
        lax.all_to_all(
            send_grad.reshape(nodes, half_cap, width),
            "node",
            split_axis=0,
            concat_axis=0,
            tiled=True,
        ),
        lax.all_to_all(
            send_gate.reshape(nodes, half_cap), "node", split_axis=0, concat_axis=0, tiled=True
        ),
    )
    other_in, other_grad, other_gate = partner((mine_in, mine_grad, mine_gate), "node", 0)
    rows_in = jnp.concatenate([mine_in, other_in], axis=1).reshape(-1, width)
    rows_grad = jnp.concatenate([mine_grad, other_grad], axis=1).reshape(-1, width)
    rows_gate = jnp.concatenate([mine_gate, other_gate], axis=1).reshape(-1).astype(jnp.float32)
    gate_mat_grad, up_mat_grad, down_grad, input_part, gate_part = expert_backward(
        rows_in, rows_grad, rows_gate, gate_mat, up_mat, down_mat
    )
    input_part = input_part.reshape(nodes, capacity, width)
    gate_part = gate_part.reshape(nodes, capacity)
    partner_input, partner_gate = partner(
        (input_part[:, half_cap:], gate_part[:, half_cap:]), "node", 0
    )
    own_input = input_part[:, :half_cap] + partner_input
    own_gate = gate_part[:, :half_cap] + partner_gate
    back_input, back_gate = (
        lax.all_to_all(own_input, "node", split_axis=0, concat_axis=0, tiled=True),
        lax.all_to_all(own_gate, "node", split_axis=0, concat_axis=0, tiled=True),
    )
    summed_input = back_input.reshape(-1, width)
    summed_gate = back_gate.reshape(-1)
    x_grad = (
        summed_input[send_place]
        .reshape(tok_rows, top_count, width)
        .sum(axis=1)
        .astype(jnp.bfloat16)
    )
    gate_grad = summed_gate[send_place].reshape(tok_rows, top_count)
    return (x_grad, gate_grad, gate_mat_grad[None], up_mat_grad[None], down_grad[None])


def ring_kernel(
    nodes,
    x_hbm,
    g_hbm,
    ids_ref,
    values_ref,
    wg_hbm,
    wu_hbm,
    wd_hbm,
    dx_hbm,
    gg_ref,
    dwg_hbm,
    dwu_hbm,
    dwd_hbm,
    tok,
    gates,
    w_mat,
    wd_mat,
    acc_in,
    acc_down,
    upstream,
    grad_pre,
    hidden,
    gate_col,
    gate_part,
    dx_part,
    pack_send,
    pack_recv,
    sum_pack_send,
    sum_pack_recv,
    home,
    own_part,
    own_gate,
    ring_sum,
    side_recv,
    side_send,
    ring_gate,
    side_gate_recv,
    side_gate_send,
    gate_rows,
    home_gate,
    dx_out,
    load_sem,
    tok_ring_send,
    tok_ring_recv,
    tok_side_send,
    tok_side_recv,
    gates_ring_send,
    gates_ring_recv,
    gates_side_send,
    gates_side_recv,
    sum_ring_send,
    sum_ring_recv,
    sum_side_send,
    sum_side_recv,
    gsum_ring_send,
    gsum_ring_recv,
    gsum_side_send,
    gsum_side_recv,
):
    chips = nodes // 2
    depth = chips // 2
    rows, width = x_hbm.shape
    lanes = 128
    tiles = wg_hbm.shape[2] // lanes
    cols = 512
    me = lax.axis_index("node")
    core = me % 2
    mate = 1 - core
    chip = me // 2
    side = chip % 2
    place = chip // 2 + side * (2 * depth - 1 - 2 * (chip // 2))

    def node_at(where):
        where = (where + chips) % chips
        row = where // depth
        level = where + row * (2 * depth - 1 - 2 * where)
        return (level * 2 + row) * 2 + core

    step_dir = 1 - 2 * core
    ahead = {"node": node_at(place + step_dir)}
    behind = {"node": node_at(place - step_dir)}
    other = {"node": chip * 2 + mate}
    chip_ahead = node_at(place + step_dir) // 2
    chip_behind = node_at(place - step_dir) // 2

    loads = [
        (x_hbm, tok.at[0, 0, core]),
        (g_hbm, tok.at[0, 1, core]),
        (wd_hbm.at[0], wd_mat),
    ]
    for j in range(tiles):
        part = pl.ds(j * lanes, lanes)
        loads.append((wg_hbm.at[0, :, part], w_mat.at[j, :, pl.ds(0, lanes)]))
        loads.append((wu_hbm.at[0, :, part], w_mat.at[j, :, pl.ds(lanes, lanes)]))
    loads = [
        pltpu.make_async_copy(source, target, load_sem.at[i])
        for i, (source, target) in enumerate(loads)
    ]
    for load in loads[:2]:
        load.start()

    barrier = pltpu.get_barrier_semaphore()
    for target in (ahead, behind, other):
        pl.semaphore_signal(barrier, inc=1, device_id=target, device_id_type=pl.DeviceIdType.MESH)
    pl.semaphore_wait(barrier, 3)

    def remote(source, target, send, recv, device):
        return pltpu.make_async_remote_copy(
            src_ref=source,
            dst_ref=target,
            send_sem=send,
            recv_sem=recv,
            device_id=device,
            device_id_type=pl.DeviceIdType.MESH,
        )

    def tok_ring(s, kind):
        return remote(
            tok.at[s, kind, core],
            tok.at[s + 1, kind, core],
            tok_ring_send.at[s, kind],
            tok_ring_recv.at[s + 1, kind],
            ahead,
        )

    limit = pack_send.shape[1]

    def select(table, expert):
        named = lax.broadcasted_iota(jnp.int32, (slots, rows), 0) == expert
        routed = jnp.where(named, table.astype(jnp.float32), 0.0) > 0.0
        mask = jnp.max(routed.astype(jnp.float32), axis=0, keepdims=True)
        before = lax.broadcasted_iota(jnp.int32, (rows, rows), 0) < lax.broadcasted_iota(
            jnp.int32, (rows, rows), 1
        )
        rank = jnp.dot(
            jnp.broadcast_to(mask, (slots, rows)).astype(jnp.bfloat16),
            before.astype(jnp.bfloat16),
            preferred_element_type=jnp.float32,
        )[:1]
        place_of = lax.broadcasted_iota(jnp.int32, (limit, rows), 0).astype(jnp.float32)
        return jnp.where(place_of == rank, mask, 0.0).astype(jnp.bfloat16)

    def packed(chooser, dense):
        return jnp.dot(chooser, dense, preferred_element_type=jnp.float32).astype(jnp.bfloat16)

    def spread(chooser, rows_packed):
        return lax.dot_general(
            chooser, rows_packed, (((0,), (0,)), ((), ())), preferred_element_type=jnp.float32
        )

    def tok_pack(kind):
        return remote(
            pack_send.at[kind],
            pack_recv.at[kind],
            tok_ring_send.at[chips - 2, kind],
            tok_ring_recv.at[chips - 1, kind],
            ahead,
        )

    def sum_pack(h):
        return remote(
            sum_pack_send.at[h],
            sum_pack_recv.at[h],
            sum_ring_send.at[1, h],
            sum_ring_recv.at[2, h],
            ahead,
        )

    def gates_ring(s):
        return remote(
            gates.at[s, core],
            gates.at[s + 1, core],
            gates_ring_send.at[s],
            gates_ring_recv.at[s + 1],
            ahead,
        )

    def tok_side(s, kind, whose):
        return remote(
            tok.at[s, kind, whose],
            tok.at[s, kind, whose],
            tok_side_send.at[s, kind],
            tok_side_recv.at[s, kind],
            other,
        )

    def gates_side(s, whose):
        return remote(
            gates.at[s, whose],
            gates.at[s, whose],
            gates_side_send.at[s],
            gates_side_recv.at[s],
            other,
        )

    half = width // 2

    def sum_ring(s, h):
        return remote(
            ring_sum.at[s, h],
            ring_sum.at[s + 1, h],
            sum_ring_send.at[s, h],
            sum_ring_recv.at[s + 1, h],
            ahead,
        )

    def gsum_ring(s):
        return remote(
            ring_gate.at[s],
            ring_gate.at[s + 1],
            gsum_ring_send.at[s],
            gsum_ring_recv.at[s + 1],
            ahead,
        )

    def sum_side(s):
        return (
            remote(
                side_send.at[s], side_recv.at[s], sum_side_send.at[s], sum_side_recv.at[s], other
            ),
            remote(
                side_gate_send.at[s],
                side_gate_recv.at[s],
                gsum_side_send.at[s],
                gsum_side_recv.at[s],
                other,
            ),
        )

    slots = gates.shape[2]
    top = ids_ref.shape[0]
    expert = lax.broadcasted_iota(jnp.int32, (slots, rows), 0)
    ids, values = ids_ref[...], values_ref[...]
    table = jnp.zeros((slots, rows), jnp.float32)
    for k in range(top):
        table = table + jnp.where(ids[k : k + 1] == expert, values[k : k + 1], 0.0)
    gates[0, core] = table.astype(jnp.bfloat16)

    for load in loads[:2]:
        load.wait()

    contract_last = (((1,), (1,)), ((), ()))
    contract_first = (((0,), (0,)), ((), ()))

    lag = 2
    kept = own_part.shape[0]

    def add_and_send(s):
        for copy in sum_side(s):
            copy.wait_recv()
        gates_total = own_gate[s % kept] + side_gate_recv[s]

        @pl.when(s == 1)
        def _():
            ring_gate[s] = gates_total

        @pl.when(s >= 2)
        def _():
            gsum_ring(s - 1).wait_recv()
            ring_gate[s] = gates_total + ring_gate[s]

        gsum_ring(s).start()
        for h in range(2):
            part = slice(h * half, (h + 1) * half)

            @pl.when(s == 1)
            def _():
                total = own_part[s % kept, h] + side_recv[s, :, part].astype(jnp.float32)
                chooser = select(gates[s, core], chip)
                sum_pack_send[h] = packed(chooser, total.astype(jnp.bfloat16))
                sum_pack(h).start()

            @pl.when(s == 2)
            def _():
                sum_pack(h).wait_recv()
                chooser = select(gates[s, core], chip_behind)
                ring_sum[s, h] = (
                    own_part[s % kept, h]
                    + side_recv[s, :, part].astype(jnp.float32)
                    + spread(chooser, sum_pack_recv[h])
                ).astype(jnp.bfloat16)

            @pl.when(s >= 3)
            def _():
                sum_ring(s - 1, h).wait_recv()
                ring_sum[s, h] = (
                    own_part[s % kept, h]
                    + side_recv[s, :, part].astype(jnp.float32)
                    + ring_sum[s, h].astype(jnp.float32)
                ).astype(jnp.bfloat16)

            @pl.when(s >= 2)
            def _():
                sum_ring(s, h).start()

    def step(s, carry):
        @pl.when(s >= 1)
        def _():
            gates_ring(s - 1).wait_recv()

        @pl.when(s < chips - 1)
        def _():
            gates_ring(s).start()

        gates_side(s, core).start()
        for kind in (1, 0):

            @pl.when((s >= 1) & (s < chips - 1))
            def _():
                tok_ring(s - 1, kind).wait_recv()

            @pl.when(s < chips - 2)
            def _():
                tok_ring(s, kind).start()

            @pl.when(s == chips - 2)
            def _():
                chooser = select(gates[s, core], chip_ahead)
                pack_send[kind] = packed(chooser, tok[s, kind, core])
                tok_pack(kind).start()

            @pl.when(s == chips - 1)
            def _():
                tok_pack(kind).wait_recv()
                chooser = select(gates[s, core], chip)
                tok[s, kind, core] = spread(chooser, pack_recv[kind]).astype(jnp.bfloat16)

            tok_side(s, kind, core).start()

        @pl.when(s == 0)
        def _():
            for load in loads[2:]:
                load.start()
            acc_in[...] = jnp.zeros_like(acc_in)
            acc_down[...] = jnp.zeros_like(acc_down)
            for load in loads[2:]:
                load.wait()

        @pl.when(s >= lag + 1)
        def _():
            add_and_send(s - lag)

        gates_side(s, mate).wait_recv()
        tok_side(s, 1, mate).wait_recv()
        tok_side(s, 0, mate).wait_recv()

        pick = (lax.broadcasted_iota(jnp.int32, (slots, lanes), 0) == chip).astype(jnp.bfloat16)
        for c in range(2):
            gate_col[c * rows : (c + 1) * rows, :] = lax.dot_general(
                gates[s, c], pick, contract_first, preferred_element_type=jnp.float32
            )
        gate = gate_col[...]

        up = lax.dot_general(
            tok[s, 1].reshape(2 * rows, width),
            wd_mat[...],
            contract_last,
            preferred_element_type=jnp.float32,
        )
        for j in range(tiles):
            upstream[j] = up[:, j * lanes : (j + 1) * lanes]
        gate_part[...] = jnp.zeros_like(gate_part)

        @pl.loop(0, tiles)
        def _(j):
            pre = jnp.dot(
                tok[s, 0].reshape(2 * rows, width), w_mat[j], preferred_element_type=jnp.float32
            )
            pre_gate, pre_up = pre[:, :lanes], pre[:, lanes:]
            sig = jax.nn.sigmoid(pre_gate)
            act = pre_gate * sig
            hid = (act * pre_up).astype(jnp.bfloat16)
            ups = upstream[j]
            gate_part[...] += hid.astype(jnp.float32) * ups
            grad_hidden = gate_col[...] * ups
            grad_pre[j, :, :lanes] = (
                grad_hidden * pre_up * sig * (1.0 + pre_gate * (1.0 - sig))
            ).astype(jnp.bfloat16)
            grad_pre[j, :, lanes:] = (grad_hidden * act).astype(jnp.bfloat16)
            hidden[j] = hid

        @pl.loop(0, width // cols)
        def _(n):
            at = pl.ds(pl.multiple_of(n * cols, cols), cols)
            total = None
            for j in range(tiles):
                term = lax.dot_general(
                    grad_pre[j], w_mat[j, at, :], contract_last, preferred_element_type=jnp.float32
                )
                total = term if total is None else total + term
            dx_part[0, :, at] = total[:rows]
            dx_part[1, :, at] = total[rows:]

        for c in range(2):
            column = jnp.sum(gate_part[c * rows : (c + 1) * rows, :], axis=1, keepdims=True)
            across = jnp.transpose(jnp.broadcast_to(column, (rows, lanes)))[:slots]
            mine = lax.broadcasted_iota(jnp.int32, (slots, rows), 0) == chip
            gate_rows[c] = jnp.where(mine, across, 0.0)

        side_send[s] = dx_part[mate].astype(jnp.bfloat16)
        side_gate_send[s] = gate_rows[mate]
        for copy in sum_side(s):
            copy.start()

        @pl.when(s == 0)
        def _():
            for h in range(2):
                home[h] = dx_part[core, :, h * half : (h + 1) * half]
            home_gate[...] = gate_rows[core]

        @pl.when(s >= 1)
        def _():
            for h in range(2):
                own_part[s % kept, h] = dx_part[core, :, h * half : (h + 1) * half]
            own_gate[s % kept] = gate_rows[core]

        @pl.when(s == chips - 1)
        def _():
            for late in range(lag - 1, 0, -1):
                add_and_send(chips - 1 - late)

        @pl.loop(0, width // cols)
        def _(n):
            at = pl.ds(pl.multiple_of(n * cols, cols), cols)
            x_tile = tok[s, 0, :, :, at].reshape(2 * rows, cols)
            g_tile = tok[s, 1, :, :, at].reshape(2 * rows, cols).astype(jnp.float32)
            scaled = jnp.concatenate(
                [
                    (g_tile[:, k * lanes : (k + 1) * lanes] * gate_col[...]).astype(jnp.bfloat16)
                    for k in range(cols // lanes)
                ],
                axis=1,
            )
            for j in range(tiles):
                acc_in[j, at, :] += lax.dot_general(
                    x_tile, grad_pre[j], contract_first, preferred_element_type=jnp.float32
                )
                acc_down[j, :, at] += lax.dot_general(
                    hidden[j], scaled, contract_first, preferred_element_type=jnp.float32
                )

        return carry

    lax.fori_loop(0, chips, step, 0)
    add_and_send(chips - 1)

    for j in range(tiles):
        w_mat[j] = acc_in[j].astype(jnp.bfloat16)
        wd_mat[j * lanes : (j + 1) * lanes, :] = acc_down[j].astype(jnp.bfloat16)
    stores = [(wd_mat, dwd_hbm.at[0])]
    for j in range(tiles):
        part = pl.ds(j * lanes, lanes)
        stores.append((w_mat.at[j, :, pl.ds(0, lanes)], dwg_hbm.at[0, :, part]))
        stores.append((w_mat.at[j, :, pl.ds(lanes, lanes)], dwu_hbm.at[0, :, part]))
    stores = [
        pltpu.make_async_copy(source, target, load_sem.at[i])
        for i, (source, target) in enumerate(stores)
    ]
    for store in stores:
        store.start()

    for copy in sum_side(0):
        copy.wait_recv()
    gsum_ring(chips - 1).wait_recv()
    gate_sums = home_gate[...] + side_gate_recv[0] + ring_gate[chips]
    for k in range(top):
        chosen = jnp.where(ids[k : k + 1] == expert, gate_sums, 0.0)
        gg_ref[k : k + 1, :] = jnp.sum(chosen, axis=0, keepdims=True)
    for h in range(2):
        part = slice(h * half, (h + 1) * half)
        sum_ring(chips - 1, h).wait_recv()
        dx_out[:, part] = (
            home[h] + side_recv[0, :, part].astype(jnp.float32) + ring_sum[chips, h].astype(jnp.float32)
        ).astype(jnp.bfloat16)
    last = [
        pltpu.make_async_copy(dx_out, dx_hbm, load_sem.at[len(stores)]),
    ]
    for store in last:
        store.start()

    def drain(s, carry):
        @pl.when(s < chips - 1)
        def _():
            gates_ring(s).wait_send()

        @pl.when(s >= 1)
        def _():
            gsum_ring(s).wait_send()

        for kind in range(2):

            @pl.when(s < chips - 2)
            def _():
                tok_ring(s, kind).wait_send()

            @pl.when(s == chips - 2)
            def _():
                tok_pack(kind).wait_send()

            @pl.when(s == 1)
            def _():
                sum_pack(kind).wait_send()

            @pl.when(s >= 2)
            def _():
                sum_ring(s, kind).wait_send()

        gates_side(s, core).wait_send()
        for kind in range(2):
            tok_side(s, kind, core).wait_send()
        for copy in sum_side(s):
            copy.wait_send()
        return carry

    lax.fori_loop(0, chips, drain, 0)
    for store in stores + last:
        store.wait()


def hand_over(*refs):
    count = len(refs) // 2
    for source, target in zip(refs[:count], refs[count:]):
        target[...] = source[...]


def ring_local(x_rows, out_grad, expert_ids, gate_values, w_gate, w_up, w_down):
    nodes = lax.axis_size("node")
    chips = nodes // 2
    rows, width = x_rows.shape
    hid = w_gate.shape[2]
    lanes = 128
    tiles = hid // lanes
    slots = (chips + 15) // 16 * 16
    capacity = 2 * max(1, 5 * rows * expert_ids.shape[1] // (8 * chips))
    limit = min(rows, (capacity + 15) // 16 * 16)
    top = expert_ids.shape[1]
    any_space = pl.BlockSpec(memory_space=pl.ANY)
    vmem_space = pl.BlockSpec(memory_space=pltpu.VMEM)
    bf16, f32 = jnp.bfloat16, jnp.float32
    dma = pltpu.SemaphoreType.DMA
    flops = 2 * nodes * rows * width * hid * 8
    results = pl.pallas_call(
        functools.partial(ring_kernel, nodes),
        out_shape=(
            jax.ShapeDtypeStruct((rows, width), bf16),
            jax.ShapeDtypeStruct((top, rows), f32),
            jax.ShapeDtypeStruct((1, width, hid), bf16),
            jax.ShapeDtypeStruct((1, width, hid), bf16),
            jax.ShapeDtypeStruct((1, hid, width), bf16),
        ),
        in_specs=[any_space] * 2 + [vmem_space] * 2 + [any_space] * 3,
        out_specs=(any_space, vmem_space) + (any_space,) * 3,
        scratch_shapes=[
            pltpu.VMEM((chips, 2, 2, rows, width), bf16),
            pltpu.VMEM((chips, 2, slots, rows), bf16),
            pltpu.VMEM((tiles, width, 2 * lanes), bf16),
            pltpu.VMEM((hid, width), bf16),
            pltpu.VMEM((tiles, width, 2 * lanes), f32),
            pltpu.VMEM((tiles, lanes, width), f32),
            pltpu.VMEM((tiles, 2 * rows, lanes), f32),
            pltpu.VMEM((tiles, 2 * rows, 2 * lanes), bf16),
            pltpu.VMEM((tiles, 2 * rows, lanes), bf16),
            pltpu.VMEM((2 * rows, lanes), f32),
            pltpu.VMEM((2 * rows, lanes), f32),
            pltpu.VMEM((2, rows, width), f32),
            pltpu.VMEM((2, limit, width), bf16),
            pltpu.VMEM((2, limit, width), bf16),
            pltpu.VMEM((2, limit, width // 2), bf16),
            pltpu.VMEM((2, limit, width // 2), bf16),
            pltpu.VMEM((2, rows, width // 2), f32),
            pltpu.VMEM((3, 2, rows, width // 2), f32),
            pltpu.VMEM((3, slots, rows), f32),
            pltpu.VMEM((chips + 1, 2, rows, width // 2), bf16),
            pltpu.VMEM((chips, rows, width), bf16),
            pltpu.VMEM((chips, rows, width), bf16),
            pltpu.VMEM((chips + 1, slots, rows), f32),
            pltpu.VMEM((chips, slots, rows), f32),
            pltpu.VMEM((chips, slots, rows), f32),
            pltpu.VMEM((2, slots, rows), f32),
            pltpu.VMEM((slots, rows), f32),
            pltpu.VMEM((rows, width), bf16),
            dma((4 + 2 * tiles,)),
        ]
        + [dma((chips + 1, 2))] * 4
        + [dma((chips + 1,))] * 4
        + [dma((chips + 1, 2))] * 2
        + [dma((chips + 1,))] * 6,
        compiler_params=pltpu.CompilerParams(
            collective_id=0, has_side_effects=True, vmem_limit_bytes=60 * 2**20
        ),
        cost_estimate=pl.CostEstimate(
            flops=flops, bytes_accessed=12 * width * hid, transcendentals=nodes * rows * hid
        ),
    )(x_rows, out_grad, expert_ids.T, gate_values.T, w_gate, w_up, w_down)
    pieces = 4
    blocks = [
        pl.BlockSpec((rows // pieces, width), lambda i: (i, 0)),
        pl.BlockSpec((top, rows), lambda i: (0, 0)),
        pl.BlockSpec((1, width // pieces, hid), lambda i: (0, i, 0)),
        pl.BlockSpec((1, width // pieces, hid), lambda i: (0, i, 0)),
        pl.BlockSpec((1, hid // pieces, width), lambda i: (0, i, 0)),
    ]
    x_grad, gate_grad, d_gate, d_up, d_down = pl.pallas_call(
        hand_over,
        grid=(pieces,),
        out_shape=tuple(jax.ShapeDtypeStruct(r.shape, r.dtype) for r in results),
        in_specs=blocks,
        out_specs=tuple(blocks),
    )(*results)
    return (x_grad, gate_grad.T, d_gate, d_up, d_down)


def solution(mesh):
    local = ring_local if mesh.shape["node"] <= RING_NODES else exchange_local
    return jax.shard_map(
        local,
        mesh=mesh,
        in_specs=(
            P(("replica", "node"), None),
            P(("replica", "node"), None),
            P(("replica", "node"), None),
            P(("replica", "node"), None),
            P("node", None, None),
            P("node", None, None),
            P("node", None, None),
        ),
        out_specs=(
            P(("replica", "node"), None),
            P(("replica", "node"), None),
            P(("replica", "node"), None, None),
            P(("replica", "node"), None, None),
            P(("replica", "node"), None, None),
        ),
        check_vma=False,
    )
```

```python
import functools

import jax
import jax.numpy as jnp
from jax import lax
from jax.experimental import pallas as pl
from jax.experimental.pallas import tpu as pltpu
from jax.sharding import PartitionSpec as P


RING_NODES = 16


def partner(value, axis, bit):
    mask = 2**bit
    pairs = [(source, source ^ mask) for source in range(lax.axis_size(axis))]
    return lax.ppermute(value, axis, pairs)


def expert_backward(rows_in, rows_grad, rows_gate, gate_mat, up_mat, down_mat):
    contract_rows = (((0,), (0,)), ((), ()))
    contract_cols = (((1,), (1,)), ((), ()))
    pre_gate = jnp.dot(rows_in, gate_mat, preferred_element_type=jnp.float32)
    pre_up = jnp.dot(rows_in, up_mat, preferred_element_type=jnp.float32)
    sigmoid_gate = jax.nn.sigmoid(pre_gate)
    activation = pre_gate * sigmoid_gate
    hidden = (activation * pre_up).astype(jnp.bfloat16)
    upstream = lax.dot_general(
        rows_grad, down_mat, contract_cols, preferred_element_type=jnp.float32
    )
    gate_part = jnp.sum(hidden.astype(jnp.float32) * upstream, axis=1)
    grad_hidden = rows_gate[:, None] * upstream
    grad_pre_gate = (
        grad_hidden * pre_up * sigmoid_gate * (1.0 + pre_gate * (1.0 - sigmoid_gate))
    ).astype(jnp.bfloat16)
    grad_pre_up = (grad_hidden * activation).astype(jnp.bfloat16)
    scaled_grad = (rows_gate[:, None] * rows_grad.astype(jnp.float32)).astype(jnp.bfloat16)
    down_grad = lax.dot_general(
        hidden, scaled_grad, contract_rows, preferred_element_type=jnp.float32
    ).astype(jnp.bfloat16)
    gate_mat_grad = lax.dot_general(
        rows_in, grad_pre_gate, contract_rows, preferred_element_type=jnp.float32
    ).astype(jnp.bfloat16)
    up_mat_grad = lax.dot_general(
        rows_in, grad_pre_up, contract_rows, preferred_element_type=jnp.float32
    ).astype(jnp.bfloat16)
    input_part = lax.dot_general(
        grad_pre_gate, gate_mat, contract_cols, preferred_element_type=jnp.float32
    )
    input_part = input_part + lax.dot_general(
        grad_pre_up, up_mat, contract_cols, preferred_element_type=jnp.float32
    )
    return (gate_mat_grad, up_mat_grad, down_grad, input_part, gate_part)


def exchange_local(x_rows, out_grad, expert_ids, gate_values, w_gate, w_up, w_down):
    nodes = lax.axis_size("node")
    experts = nodes // 2
    tok_rows, width = x_rows.shape
    top_count = expert_ids.shape[1]
    capacity = 2 * max(1, 5 * tok_rows * top_count // (8 * experts))
    half_cap = capacity // 2
    flat_ids = expert_ids.reshape(-1)
    one_hot = (flat_ids[:, None] == jnp.arange(experts, dtype=jnp.int32)[None, :]).astype(jnp.int32)
    earlier = jnp.cumsum(one_hot, axis=0) - one_hot
    slot_index = jnp.sum(earlier * one_hot, axis=1)
    send_place = flat_ids * capacity + slot_index
    send_in = (
        jnp.zeros((experts * capacity, width), jnp.bfloat16)
        .at[send_place]
        .set(jnp.repeat(x_rows, top_count, axis=0))
    )
    send_grad = (
        jnp.zeros((experts * capacity, width), jnp.bfloat16)
        .at[send_place]
        .set(jnp.repeat(out_grad, top_count, axis=0))
    )
    send_gate = (
        jnp.zeros((experts * capacity,), jnp.bfloat16)
        .at[send_place]
        .set(gate_values.reshape(-1).astype(jnp.bfloat16))
    )
    gate_mat = w_gate[0]
    up_mat = w_up[0]
    down_mat = w_down[0]
    mine_in, mine_grad, mine_gate = (
        lax.all_to_all(
            send_in.reshape(nodes, half_cap, width), "node", split_axis=0, concat_axis=0, tiled=True
        ),
        lax.all_to_all(
            send_grad.reshape(nodes, half_cap, width),
            "node",
            split_axis=0,
            concat_axis=0,
            tiled=True,
        ),
        lax.all_to_all(
            send_gate.reshape(nodes, half_cap), "node", split_axis=0, concat_axis=0, tiled=True
        ),
    )
    other_in, other_grad, other_gate = partner((mine_in, mine_grad, mine_gate), "node", 0)
    rows_in = jnp.concatenate([mine_in, other_in], axis=1).reshape(-1, width)
    rows_grad = jnp.concatenate([mine_grad, other_grad], axis=1).reshape(-1, width)
    rows_gate = jnp.concatenate([mine_gate, other_gate], axis=1).reshape(-1).astype(jnp.float32)
    gate_mat_grad, up_mat_grad, down_grad, input_part, gate_part = expert_backward(
        rows_in, rows_grad, rows_gate, gate_mat, up_mat, down_mat
    )
    input_part = input_part.reshape(nodes, capacity, width)
    gate_part = gate_part.reshape(nodes, capacity)
    partner_input, partner_gate = partner(
        (input_part[:, half_cap:], gate_part[:, half_cap:]), "node", 0
    )
    own_input = input_part[:, :half_cap] + partner_input
    own_gate = gate_part[:, :half_cap] + partner_gate
    back_input, back_gate = (
        lax.all_to_all(own_input, "node", split_axis=0, concat_axis=0, tiled=True),
        lax.all_to_all(own_gate, "node", split_axis=0, concat_axis=0, tiled=True),
    )
    summed_input = back_input.reshape(-1, width)
    summed_gate = back_gate.reshape(-1)
    x_grad = (
        summed_input[send_place]
        .reshape(tok_rows, top_count, width)
        .sum(axis=1)
        .astype(jnp.bfloat16)
    )
    gate_grad = summed_gate[send_place].reshape(tok_rows, top_count)
    return (x_grad, gate_grad, gate_mat_grad[None], up_mat_grad[None], down_grad[None])


def ring_kernel(
    nodes,
    x_hbm,
    g_hbm,
    ids_ref,
    values_ref,
    wg_hbm,
    wu_hbm,
    wd_hbm,
    dx_hbm,
    gg_ref,
    dwg_hbm,
    dwu_hbm,
    dwd_hbm,
    tok,
    gates,
    w_mat,
    wd_mat,
    acc_in,
    acc_down,
    upstream,
    grad_pre,
    hidden,
    gate_col,
    gate_part,
    dx_part,
    pack_send,
    pack_recv,
    sum_pack_send,
    sum_pack_recv,
    home,
    own_part,
    own_gate,
    ring_sum,
    side_recv,
    side_send,
    ring_gate,
    side_gate_recv,
    side_gate_send,
    gate_rows,
    home_gate,
    dx_out,
    load_sem,
    tok_ring_send,
    tok_ring_recv,
    tok_side_send,
    tok_side_recv,
    gates_ring_send,
    gates_ring_recv,
    gates_side_send,
    gates_side_recv,
    sum_ring_send,
    sum_ring_recv,
    sum_side_send,
    sum_side_recv,
    gsum_ring_send,
    gsum_ring_recv,
    gsum_side_send,
    gsum_side_recv,
):
    chips = nodes // 2
    depth = chips // 2
    rows, width = x_hbm.shape
    lanes = 128
    tiles = wg_hbm.shape[2] // lanes
    cols = 512
    me = lax.axis_index("node")
    core = me % 2
    mate = 1 - core
    chip = me // 2
    side = chip % 2
    place = chip // 2 + side * (2 * depth - 1 - 2 * (chip // 2))

    def node_at(where):
        where = (where + chips) % chips
        row = where // depth
        level = where + row * (2 * depth - 1 - 2 * where)
        return (level * 2 + row) * 2 + core

    step_dir = 1 - 2 * core
    ahead = {"node": node_at(place + step_dir)}
    behind = {"node": node_at(place - step_dir)}
    other = {"node": chip * 2 + mate}
    chip_ahead = node_at(place + step_dir) // 2
    chip_behind = node_at(place - step_dir) // 2

    loads = [
        (x_hbm, tok.at[0, 0, core]),
        (g_hbm, tok.at[0, 1, core]),
        (wd_hbm.at[0], wd_mat),
    ]
    for j in range(tiles):
        part = pl.ds(j * lanes, lanes)
        loads.append((wg_hbm.at[0, :, part], w_mat.at[j, :, pl.ds(0, lanes)]))
        loads.append((wu_hbm.at[0, :, part], w_mat.at[j, :, pl.ds(lanes, lanes)]))
    loads = [
        pltpu.make_async_copy(source, target, load_sem.at[i])
        for i, (source, target) in enumerate(loads)
    ]
    for load in loads[:2]:
        load.start()

    barrier = pltpu.get_barrier_semaphore()
    for target in (ahead, behind, other):
        pl.semaphore_signal(barrier, inc=1, device_id=target, device_id_type=pl.DeviceIdType.MESH)
    pl.semaphore_wait(barrier, 3)

    def remote(source, target, send, recv, device):
        return pltpu.make_async_remote_copy(
            src_ref=source,
            dst_ref=target,
            send_sem=send,
            recv_sem=recv,
            device_id=device,
            device_id_type=pl.DeviceIdType.MESH,
        )

    def tok_ring(s, kind):
        return remote(
            tok.at[s, kind, core],
            tok.at[s + 1, kind, core],
            tok_ring_send.at[s, kind],
            tok_ring_recv.at[s + 1, kind],
            ahead,
        )

    limit = pack_send.shape[1]

    def select(table, expert):
        named = lax.broadcasted_iota(jnp.int32, (slots, rows), 0) == expert
        routed = jnp.where(named, table.astype(jnp.float32), 0.0) > 0.0
        mask = jnp.max(routed.astype(jnp.float32), axis=0, keepdims=True)
        before = lax.broadcasted_iota(jnp.int32, (rows, rows), 0) < lax.broadcasted_iota(
            jnp.int32, (rows, rows), 1
        )
        rank = jnp.dot(
            jnp.broadcast_to(mask, (slots, rows)).astype(jnp.bfloat16),
            before.astype(jnp.bfloat16),
            preferred_element_type=jnp.float32,
        )[:1]
        place_of = lax.broadcasted_iota(jnp.int32, (limit, rows), 0).astype(jnp.float32)
        return jnp.where(place_of == rank, mask, 0.0).astype(jnp.bfloat16)

    def packed(chooser, dense):
        return jnp.dot(chooser, dense, preferred_element_type=jnp.float32).astype(jnp.bfloat16)

    def spread(chooser, rows_packed):
        return lax.dot_general(
            chooser, rows_packed, (((0,), (0,)), ((), ())), preferred_element_type=jnp.float32
        )

    def tok_pack(kind):
        return remote(
            pack_send.at[kind],
            pack_recv.at[kind],
            tok_ring_send.at[chips - 2, kind],
            tok_ring_recv.at[chips - 1, kind],
            ahead,
        )

    def sum_pack(h):
        return remote(
            sum_pack_send.at[h],
            sum_pack_recv.at[h],
            sum_ring_send.at[1, h],
            sum_ring_recv.at[2, h],
            ahead,
        )

    def gates_ring(s):
        return remote(
            gates.at[s, core],
            gates.at[s + 1, core],
            gates_ring_send.at[s],
            gates_ring_recv.at[s + 1],
            ahead,
        )

    def tok_side(s, kind, whose):
        return remote(
            tok.at[s, kind, whose],
            tok.at[s, kind, whose],
            tok_side_send.at[s, kind],
            tok_side_recv.at[s, kind],
            other,
        )

    def gates_side(s, whose):
        return remote(
            gates.at[s, whose],
            gates.at[s, whose],
            gates_side_send.at[s],
            gates_side_recv.at[s],
            other,
        )

    half = width // 2

    def sum_ring(s, h):
        return remote(
            ring_sum.at[s, h],
            ring_sum.at[s + 1, h],
            sum_ring_send.at[s, h],
            sum_ring_recv.at[s + 1, h],
            ahead,
        )

    def gsum_ring(s):
        return remote(
            ring_gate.at[s],
            ring_gate.at[s + 1],
            gsum_ring_send.at[s],
            gsum_ring_recv.at[s + 1],
            ahead,
        )

    def sum_side(s):
        return (
            remote(
                side_send.at[s], side_recv.at[s], sum_side_send.at[s], sum_side_recv.at[s], other
            ),
            remote(
                side_gate_send.at[s],
                side_gate_recv.at[s],
                gsum_side_send.at[s],
                gsum_side_recv.at[s],
                other,
            ),
        )

    slots = gates.shape[2]
    top = ids_ref.shape[0]
    expert = lax.broadcasted_iota(jnp.int32, (slots, rows), 0)
    ids, values = ids_ref[...], values_ref[...]
    table = jnp.zeros((slots, rows), jnp.float32)
    for k in range(top):
        table = table + jnp.where(ids[k : k + 1] == expert, values[k : k + 1], 0.0)
    gates[0, core] = table.astype(jnp.bfloat16)

    for load in loads[:2]:
        load.wait()

    contract_last = (((1,), (1,)), ((), ()))
    contract_first = (((0,), (0,)), ((), ()))

    lag = 2
    kept = own_part.shape[0]

    def add_and_send(s):
        for copy in sum_side(s):
            copy.wait_recv()
        gates_total = own_gate[s % kept] + side_gate_recv[s]

        @pl.when(s == 1)
        def _():
            ring_gate[s] = gates_total

        @pl.when(s >= 2)
        def _():
            gsum_ring(s - 1).wait_recv()
            ring_gate[s] = gates_total + ring_gate[s]

        gsum_ring(s).start()
        for h in range(2):
            part = slice(h * half, (h + 1) * half)

            @pl.when(s == 1)
            def _():
                total = own_part[s % kept, h] + side_recv[s, :, part].astype(jnp.float32)
                chooser = select(gates[s, core], chip)
                sum_pack_send[h] = packed(chooser, total.astype(jnp.bfloat16))
                sum_pack(h).start()

            @pl.when(s == 2)
            def _():
                sum_pack(h).wait_recv()
                chooser = select(gates[s, core], chip_behind)
                ring_sum[s, h] = (
                    own_part[s % kept, h]
                    + side_recv[s, :, part].astype(jnp.float32)
                    + spread(chooser, sum_pack_recv[h])
                ).astype(jnp.bfloat16)

            @pl.when(s >= 3)
            def _():
                sum_ring(s - 1, h).wait_recv()
                ring_sum[s, h] = (
                    own_part[s % kept, h]
                    + side_recv[s, :, part].astype(jnp.float32)
                    + ring_sum[s, h].astype(jnp.float32)
                ).astype(jnp.bfloat16)

            @pl.when(s >= 2)
            def _():
                sum_ring(s, h).start()

    def step(s, carry):
        @pl.when(s >= 1)
        def _():
            gates_ring(s - 1).wait_recv()

        @pl.when(s < chips - 1)
        def _():
            gates_ring(s).start()

        gates_side(s, core).start()
        for kind in (1, 0):

            @pl.when((s >= 1) & (s < chips - 1))
            def _():
                tok_ring(s - 1, kind).wait_recv()

            @pl.when(s < chips - 2)
            def _():
                tok_ring(s, kind).start()

            @pl.when(s == chips - 2)
            def _():
                chooser = select(gates[s, core], chip_ahead)
                pack_send[kind] = packed(chooser, tok[s, kind, core])
                tok_pack(kind).start()

            @pl.when(s == chips - 1)
            def _():
                tok_pack(kind).wait_recv()
                chooser = select(gates[s, core], chip)
                tok[s, kind, core] = spread(chooser, pack_recv[kind]).astype(jnp.bfloat16)

            tok_side(s, kind, core).start()

        @pl.when(s == 0)
        def _():
            for load in loads[2:]:
                load.start()
            acc_in[...] = jnp.zeros_like(acc_in)
            acc_down[...] = jnp.zeros_like(acc_down)
            for load in loads[2:]:
                load.wait()

        @pl.when(s >= lag + 1)
        def _():
            add_and_send(s - lag)

        gates_side(s, mate).wait_recv()
        tok_side(s, 1, mate).wait_recv()
        tok_side(s, 0, mate).wait_recv()

        pick = (lax.broadcasted_iota(jnp.int32, (slots, lanes), 0) == chip).astype(jnp.bfloat16)
        for c in range(2):
            gate_col[c * rows : (c + 1) * rows, :] = lax.dot_general(
                gates[s, c], pick, contract_first, preferred_element_type=jnp.float32
            )
        gate = gate_col[...]

        up = lax.dot_general(
            tok[s, 1].reshape(2 * rows, width),
            wd_mat[...],
            contract_last,
            preferred_element_type=jnp.float32,
        )
        for j in range(tiles):
            upstream[j] = up[:, j * lanes : (j + 1) * lanes]
        gate_part[...] = jnp.zeros_like(gate_part)

        @pl.loop(0, tiles)
        def _(j):
            pre = jnp.dot(
                tok[s, 0].reshape(2 * rows, width), w_mat[j], preferred_element_type=jnp.float32
            )
            pre_gate, pre_up = pre[:, :lanes], pre[:, lanes:]
            sig = jax.nn.sigmoid(pre_gate)
            act = pre_gate * sig
            hid = (act * pre_up).astype(jnp.bfloat16)
            ups = upstream[j]
            gate_part[...] += hid.astype(jnp.float32) * ups
            grad_hidden = gate_col[...] * ups
            grad_pre[j, :, :lanes] = (
                grad_hidden * pre_up * sig * (1.0 + pre_gate * (1.0 - sig))
            ).astype(jnp.bfloat16)
            grad_pre[j, :, lanes:] = (grad_hidden * act).astype(jnp.bfloat16)
            hidden[j] = hid

        @pl.loop(0, width // cols)
        def _(n):
            at = pl.ds(pl.multiple_of(n * cols, cols), cols)
            total = None
            for j in range(tiles):
                term = lax.dot_general(
                    grad_pre[j], w_mat[j, at, :], contract_last, preferred_element_type=jnp.float32
                )
                total = term if total is None else total + term
            dx_part[0, :, at] = total[:rows]
            dx_part[1, :, at] = total[rows:]

        for c in range(2):
            column = jnp.sum(gate_part[c * rows : (c + 1) * rows, :], axis=1, keepdims=True)
            across = jnp.transpose(jnp.broadcast_to(column, (rows, lanes)))[:slots]
            mine = lax.broadcasted_iota(jnp.int32, (slots, rows), 0) == chip
            gate_rows[c] = jnp.where(mine, across, 0.0)

        side_send[s] = dx_part[mate].astype(jnp.bfloat16)
        side_gate_send[s] = gate_rows[mate]
        for copy in sum_side(s):
            copy.start()

        @pl.when(s == 0)
        def _():
            for h in range(2):
                home[h] = dx_part[core, :, h * half : (h + 1) * half]
            home_gate[...] = gate_rows[core]

        @pl.when(s >= 1)
        def _():
            for h in range(2):
                own_part[s % kept, h] = dx_part[core, :, h * half : (h + 1) * half]
            own_gate[s % kept] = gate_rows[core]

        @pl.when(s == chips - 1)
        def _():
            for late in range(lag - 1, 0, -1):
                add_and_send(chips - 1 - late)

        @pl.loop(0, width // cols)
        def _(n):
            at = pl.ds(pl.multiple_of(n * cols, cols), cols)
            x_tile = tok[s, 0, :, :, at].reshape(2 * rows, cols)
            g_tile = tok[s, 1, :, :, at].reshape(2 * rows, cols).astype(jnp.float32)
            scaled = jnp.concatenate(
                [
                    (g_tile[:, k * lanes : (k + 1) * lanes] * gate_col[...]).astype(jnp.bfloat16)
                    for k in range(cols // lanes)
                ],
                axis=1,
            )
            for j in range(tiles):
                acc_in[j, at, :] += lax.dot_general(
                    x_tile, grad_pre[j], contract_first, preferred_element_type=jnp.float32
                )
                acc_down[j, :, at] += lax.dot_general(
                    hidden[j], scaled, contract_first, preferred_element_type=jnp.float32
                )

        return carry

    lax.fori_loop(0, chips, step, 0)
    add_and_send(chips - 1)

    for j in range(tiles):
        w_mat[j] = acc_in[j].astype(jnp.bfloat16)
        wd_mat[j * lanes : (j + 1) * lanes, :] = acc_down[j].astype(jnp.bfloat16)
    stores = [(wd_mat, dwd_hbm.at[0])]
    for j in range(tiles):
        part = pl.ds(j * lanes, lanes)
        stores.append((w_mat.at[j, :, pl.ds(0, lanes)], dwg_hbm.at[0, :, part]))
        stores.append((w_mat.at[j, :, pl.ds(lanes, lanes)], dwu_hbm.at[0, :, part]))
    stores = [
        pltpu.make_async_copy(source, target, load_sem.at[i])
        for i, (source, target) in enumerate(stores)
    ]
    for store in stores:
        store.start()

    for copy in sum_side(0):
        copy.wait_recv()
    gsum_ring(chips - 1).wait_recv()
    gate_sums = home_gate[...] + side_gate_recv[0] + ring_gate[chips]
    for k in range(top):
        chosen = jnp.where(ids[k : k + 1] == expert, gate_sums, 0.0)
        gg_ref[k : k + 1, :] = jnp.sum(chosen, axis=0, keepdims=True)
    for h in range(2):
        part = slice(h * half, (h + 1) * half)
        sum_ring(chips - 1, h).wait_recv()
        dx_out[:, part] = (
            home[h] + side_recv[0, :, part].astype(jnp.float32) + ring_sum[chips, h].astype(jnp.float32)
        ).astype(jnp.bfloat16)
    last = [
        pltpu.make_async_copy(dx_out, dx_hbm, load_sem.at[len(stores)]),
    ]
    for store in last:
        store.start()

    def drain(s, carry):
        @pl.when(s < chips - 1)
        def _():
            gates_ring(s).wait_send()

        @pl.when(s >= 1)
        def _():
            gsum_ring(s).wait_send()

        for kind in range(2):

            @pl.when(s < chips - 2)
            def _():
                tok_ring(s, kind).wait_send()

            @pl.when(s == chips - 2)
            def _():
                tok_pack(kind).wait_send()

            @pl.when(s == 1)
            def _():
                sum_pack(kind).wait_send()

            @pl.when(s >= 2)
            def _():
                sum_ring(s, kind).wait_send()

        gates_side(s, core).wait_send()
        for kind in range(2):
            tok_side(s, kind, core).wait_send()
        for copy in sum_side(s):
            copy.wait_send()
        return carry

    lax.fori_loop(0, chips, drain, 0)
    for store in stores + last:
        store.wait()


def hand_over(*refs):
    count = len(refs) // 2
    for source, target in zip(refs[:count], refs[count:]):
        target[...] = source[...]


def ring_local(x_rows, out_grad, expert_ids, gate_values, w_gate, w_up, w_down):
    nodes = lax.axis_size("node")
    chips = nodes // 2
    rows, width = x_rows.shape
    hid = w_gate.shape[2]
    lanes = 128
    tiles = hid // lanes
    slots = (chips + 15) // 16 * 16
    capacity = 2 * max(1, 5 * rows * expert_ids.shape[1] // (8 * chips))
    limit = min(rows, (capacity + 15) // 16 * 16)
    top = expert_ids.shape[1]
    any_space = pl.BlockSpec(memory_space=pl.ANY)
    vmem_space = pl.BlockSpec(memory_space=pltpu.VMEM)
    bf16, f32 = jnp.bfloat16, jnp.float32
    dma = pltpu.SemaphoreType.DMA
    flops = 2 * nodes * rows * width * hid * 8
    results = pl.pallas_call(
        functools.partial(ring_kernel, nodes),
        out_shape=(
            jax.ShapeDtypeStruct((rows, width), bf16),
            jax.ShapeDtypeStruct((top, rows), f32),
            jax.ShapeDtypeStruct((1, width, hid), bf16),
            jax.ShapeDtypeStruct((1, width, hid), bf16),
            jax.ShapeDtypeStruct((1, hid, width), bf16),
        ),
        in_specs=[any_space] * 2 + [vmem_space] * 2 + [any_space] * 3,
        out_specs=(any_space, vmem_space) + (any_space,) * 3,
        scratch_shapes=[
            pltpu.VMEM((chips, 2, 2, rows, width), bf16),
            pltpu.VMEM((chips, 2, slots, rows), bf16),
            pltpu.VMEM((tiles, width, 2 * lanes), bf16),
            pltpu.VMEM((hid, width), bf16),
            pltpu.VMEM((tiles, width, 2 * lanes), f32),
            pltpu.VMEM((tiles, lanes, width), f32),
            pltpu.VMEM((tiles, 2 * rows, lanes), f32),
            pltpu.VMEM((tiles, 2 * rows, 2 * lanes), bf16),
            pltpu.VMEM((tiles, 2 * rows, lanes), bf16),
            pltpu.VMEM((2 * rows, lanes), f32),
            pltpu.VMEM((2 * rows, lanes), f32),
            pltpu.VMEM((2, rows, width), f32),
            pltpu.VMEM((2, limit, width), bf16),
            pltpu.VMEM((2, limit, width), bf16),
            pltpu.VMEM((2, limit, width // 2), bf16),
            pltpu.VMEM((2, limit, width // 2), bf16),
            pltpu.VMEM((2, rows, width // 2), f32),
            pltpu.VMEM((3, 2, rows, width // 2), f32),
            pltpu.VMEM((3, slots, rows), f32),
            pltpu.VMEM((chips + 1, 2, rows, width // 2), bf16),
            pltpu.VMEM((chips, rows, width), bf16),
            pltpu.VMEM((chips, rows, width), bf16),
            pltpu.VMEM((chips + 1, slots, rows), f32),
            pltpu.VMEM((chips, slots, rows), f32),
            pltpu.VMEM((chips, slots, rows), f32),
            pltpu.VMEM((2, slots, rows), f32),
            pltpu.VMEM((slots, rows), f32),
            pltpu.VMEM((rows, width), bf16),
            dma((4 + 2 * tiles,)),
        ]
        + [dma((chips + 1, 2))] * 4
        + [dma((chips + 1,))] * 4
        + [dma((chips + 1, 2))] * 2
        + [dma((chips + 1,))] * 6,
        compiler_params=pltpu.CompilerParams(
            collective_id=0, has_side_effects=True, vmem_limit_bytes=60 * 2**20
        ),
        cost_estimate=pl.CostEstimate(
            flops=flops, bytes_accessed=12 * width * hid, transcendentals=nodes * rows * hid
        ),
    )(x_rows, out_grad, expert_ids.T, gate_values.T, w_gate, w_up, w_down)
    pieces = 2
    blocks = [
        pl.BlockSpec((rows // pieces, width), lambda i: (i, 0)),
        pl.BlockSpec((top, rows), lambda i: (0, 0)),
        pl.BlockSpec((1, width // pieces, hid), lambda i: (0, i, 0)),
        pl.BlockSpec((1, width // pieces, hid), lambda i: (0, i, 0)),
        pl.BlockSpec((1, hid // pieces, width), lambda i: (0, i, 0)),
    ]
    x_grad, gate_grad, d_gate, d_up, d_down = pl.pallas_call(
        hand_over,
        grid=(pieces,),
        out_shape=tuple(jax.ShapeDtypeStruct(r.shape, r.dtype) for r in results),
        in_specs=blocks,
        out_specs=tuple(blocks),
    )(*results)
    return (x_grad, gate_grad.T, d_gate, d_up, d_down)


def solution(mesh):
    local = ring_local if mesh.shape["node"] <= RING_NODES else exchange_local
    return jax.shard_map(
        local,
        mesh=mesh,
        in_specs=(
            P(("replica", "node"), None),
            P(("replica", "node"), None),
            P(("replica", "node"), None),
            P(("replica", "node"), None),
            P("node", None, None),
            P("node", None, None),
            P("node", None, None),
        ),
        out_specs=(
            P(("replica", "node"), None),
            P(("replica", "node"), None),
            P(("replica", "node"), None, None),
            P(("replica", "node"), None, None),
            P(("replica", "node"), None, None),
        ),
        check_vma=False,
    )
```
